32 devices in a mesh: dp: 8 (over y, x, core), mp: 4 (over z).
Axes of the slice: x: 2, y: 2, z: 4, core: 2. Of those that a mesh axis runs over, the one named last changes fastest.
Arguments:
- query_hidden: bfloat16 [4096, 4096], P('dp'), may hold values from -6 to 6
- passage_hidden: bfloat16 [4096, 4096], P('dp'), may hold values from -6 to 6
- head_weight: bfloat16 [4096, 4096], P(None, 'mp'), may hold values from -0.09375 to 0.09375
- neg_blocks: int32 [32, 4], P('dp'), may hold values from 0 to 31, as said below
- pos_ids: int32 [4096], P('dp'), may hold values from 0 to 127
Outputs:
- query_loss: float32 [4096], P('dp')
- grad_weight: float32 [4096, 4096], P('dp', 'mp')
- grad_query_hidden: bfloat16 [4096, 4096], P('dp', 'mp')
- grad_passage_hidden: bfloat16 [4096, 4096], P('dp', 'mp')
The draws below stay inside these ranges and needn't reach their ends.
Inputs may be any that keep to these rules, and one draw needn't show every extreme that they name: `neg_blocks`: within each aligned group of 4 query blocks all 16 ids are different, and at most 2 of them fall into any one aligned group of 4 passage block ids; some group of passage blocks receives exactly 2 of them.
All inputs are finite; a program needn't handle non-finite values.
Results may differ from the reference program's by a relative error of at most 0.017.
Values may be sent and summed in bfloat16 or wider, within the bound.
No kernel may reach another device: no remote copies, remote signals or barrier semaphores. Data moves between devices by JAX's collectives and lax.ppermute only.
A program may use at most 128 MiB of HBM per device.

```python
import jax
import jax.numpy as jnp
from jax import lax

D = 4096
BLK = 128
K = 4
QB_DEV = 4
NQB = 32
NQ = 4096
CAP = 2
N_MP = 4


def draw_neg_blocks(key, part):
    device_count = NQB // QB_DEV
    slot_count = device_count * CAP
    request_count = QB_DEV * K
    first_key = jax.random.fold_in(key, 11)
    second_key = jax.random.fold_in(key, 23)
    ranking = jax.random.randint(first_key, (device_count, slot_count), 0, 1048576, dtype=jnp.int32)
    ranking = ranking * slot_count + jnp.arange(slot_count, dtype=jnp.int32)[None, :]
    chosen_slots = jnp.argsort(ranking, axis=1, stable=True)[:, :request_count].astype(jnp.int32)
    owners = chosen_slots // CAP
    within = chosen_slots % CAP
    offsets = jax.random.randint(second_key, (device_count, device_count), 0, QB_DEV, dtype=jnp.int32)
    base_local = jnp.take_along_axis(offsets, owners, axis=1)
    local_ids = (base_local + within) % QB_DEV
    block_ids = owners * QB_DEV + local_ids
    return block_ids.reshape(NQB, K).astype(jnp.int32)


def place_ends(result, key, low, high):
    longest = result.shape.index(max(result.shape))
    spots = []
    for shift in (0, 1):
        where = [jax.random.randint(jax.random.fold_in(key, axis), (), 0, length) for axis, length in enumerate(result.shape)]
        where[longest] = (where[longest] + shift) % result.shape[longest]
        spots.append(tuple(where))
    return result.at[spots[0]].set(low).at[spots[1]].set(high)


def spiked(drawn, own_key, source, target, blocks, factor):
    def block_of(axis_at):
        return (jnp.arange(drawn.shape[axis_at]) // (drawn.shape[axis_at] // blocks)).reshape((-1,) + (1,) * (drawn.ndim - 1 - axis_at))

    one_side = jax.random.permutation(own_key, blocks)[block_of(target)]
    second = (block_of(target) + blocks // 2) % blocks
    return jnp.where((block_of(source) == one_side) | (block_of(source) == second), factor * drawn, drawn)


def levels(stream_key, dims, cuts, smallest, largest):
    def one(dim, shards_of):
        heights = jax.random.uniform(jax.random.fold_in(jax.random.fold_in(stream_key, 6), dim), (shards_of,), jnp.float32, smallest / len(cuts), largest / len(cuts))
        return jnp.repeat(jnp.exp(heights), dims[dim] // shards_of).reshape((-1,) + (1,) * (len(dims) - dim - 1))

    level = one(*cuts[0])
    for cut in cuts[1:]:
        level = level * one(*cut)
    return level


def noise(key, dims, deviation, reach, pieces=(), kind=jnp.bfloat16):
    drawn = deviation * jax.random.normal(key, dims, jnp.float32)
    if pieces:
        drawn = drawn * levels(key, dims, pieces, -0.22, 0.18)
    return jnp.clip(drawn, -reach, reach).astype(kind)


def gaussian_with(own_key, shape, scale, most, cuts, heavy, kind=jnp.bfloat16):
    values = scale * jax.random.normal(own_key, shape, jnp.float32)
    if cuts:
        values = values * levels(own_key, shape, cuts, -0.22, 0.18)
    return jnp.clip(spiked(values, jax.random.fold_in(own_key, 3), *heavy), -most, most).astype(kind)


def setup_inputs(seed: int = 0) -> dict:
    streams_of = jax.random.split(jax.random.key(seed), 6)
    return {
        "query_hidden": gaussian_with(streams_of[0], (NQ, D), 1.0, 6.0, ((0, 8),), (0, 1, 8, 2.0)),
        "passage_hidden": gaussian_with(streams_of[1], (NQ, D), 1.0, 6.0, ((0, 8),), (0, 1, 8, 2.0)),
        "head_weight": noise(streams_of[2], (D, D), D ** -0.5, 0.09375, ((1, 4),)),
        "neg_blocks": draw_neg_blocks(jax.random.fold_in(streams_of[5], 71), 0),
        "pos_ids": place_ends(jax.random.randint(streams_of[4], (NQ,), 0, BLK), jax.random.fold_in(streams_of[4], 1), 0, BLK - 1).astype(jnp.int32),
    }


logit_divisor = 0.02
epsilon = 1e-06

def normalize(embedding):
    inverse = lax.rsqrt(lax.optimization_barrier(jnp.sum(embedding * embedding, axis=1)) + epsilon)
    return (inverse, embedding * inverse[:, None])

def back_norm(inverse, unit_rows, d_unit):
    inner = lax.optimization_barrier(jnp.sum(unit_rows * d_unit, axis=1))
    return (inverse[:, None] * (d_unit - unit_rows * inner[:, None])).astype(jnp.bfloat16)

def input_gradient(d_embed, head_weight):
    group_width = D // N_MP
    summed = jnp.zeros((d_embed.shape[0], D), jnp.float32)
    for group in range(N_MP):
        lower = group * group_width
        grad_slice = d_embed[:, lower:lower + group_width]
        weight_slice = head_weight[:, lower:lower + group_width]
        partial_sum = jnp.dot(grad_slice, weight_slice.T, preferred_element_type=jnp.float32)
        rounded = lax.optimization_barrier(partial_sum.astype(jnp.bfloat16))
        summed = summed + rounded.astype(jnp.float32)
    return summed.astype(jnp.bfloat16)

def reference(query_hidden, passage_hidden, head_weight, neg_blocks, pos_ids):
    query_embed = jnp.dot(query_hidden, head_weight, preferred_element_type=jnp.float32)
    passage_embed = jnp.dot(passage_hidden, head_weight, preferred_element_type=jnp.float32)
    query_inv, query_unit = normalize(query_embed)
    passage_inv, passage_unit = normalize(passage_embed)
    query_norm = query_unit.astype(jnp.bfloat16)
    passage_norm = passage_unit.astype(jnp.bfloat16)
    query_blocks = query_norm.reshape(NQB, BLK, D)
    passage_blocks = passage_norm.reshape(NQB, BLK, D)
    block_lists = jnp.concatenate([jnp.arange(NQB, dtype=jnp.int32)[:, None], neg_blocks.astype(jnp.int32)], axis=1)
    positions = pos_ids.astype(jnp.int32).reshape(NQB, BLK)
    columns = jnp.arange((1 + K) * BLK, dtype=jnp.int32)

    def visit(d_passage, inputs):
        request_vectors, chosen, target = inputs
        retrieved_documents = jnp.take(passage_blocks, chosen, axis=0).reshape((1 + K) * BLK, D)
        similarity_table = jnp.dot(request_vectors, retrieved_documents.T, preferred_element_type=jnp.float32) / logit_divisor
        matching_document_slot = (columns[None, :] == target[:, None]).astype(jnp.float32)
        exponent_values = jnp.exp(similarity_table)
        normalizer_totals = lax.optimization_barrier(jnp.sum(exponent_values, axis=1))
        losses = jnp.log(normalizer_totals) - lax.optimization_barrier(jnp.sum(similarity_table * matching_document_slot, axis=1))
        attention_probabilities = ((exponent_values / normalizer_totals[:, None] - matching_document_slot) / logit_divisor).astype(jnp.bfloat16)
        d_query = jnp.dot(attention_probabilities, retrieved_documents, preferred_element_type=jnp.float32)
        d_cand = jnp.dot(attention_probabilities.T, request_vectors, preferred_element_type=jnp.float32).reshape(1 + K, BLK, D)
        rounded = lax.optimization_barrier(d_cand[1:].astype(jnp.bfloat16)).astype(jnp.float32)
        d_passage = d_passage.at[chosen[0]].add(d_cand[0])
        d_passage = d_passage.at[chosen[1:]].add(rounded)
        return (d_passage, (losses, d_query))
    start_grad = jnp.zeros((NQB, BLK, D), jnp.float32)
    d_passage, (losses, d_query) = lax.scan(visit, start_grad, (query_blocks, block_lists, positions))
    query_loss = losses.reshape(NQ)
    d_query_embed = back_norm(query_inv, query_unit, d_query.reshape(NQ, D))
    d_passage_embed = back_norm(passage_inv, passage_unit, d_passage.reshape(NQ, D))
    grad_weight = jnp.dot(query_hidden.T, d_query_embed, preferred_element_type=jnp.float32)
    grad_weight = grad_weight + jnp.dot(passage_hidden.T, d_passage_embed, preferred_element_type=jnp.float32)
    grad_query_hidden = input_gradient(d_query_embed, head_weight)
    grad_passage_hidden = input_gradient(d_passage_embed, head_weight)
    return (query_loss, grad_weight, grad_query_hidden, grad_passage_hidden)
```

```python
import functools

import jax
import jax.numpy as jnp
from jax import lax
from jax.experimental import pallas as pl
from jax.experimental.pallas import tpu as pltpu
from jax.sharding import PartitionSpec as P

logit_divisor = 0.02
epsilon = 1e-06
f32 = jnp.float32
bf16 = jnp.bfloat16
VMEM_LIMIT = 50 * 1024 * 1024
EXT = 16
NT = (((1,), (1,)), ((), ()))
NN = (((1,), (0,)), ((), ()))
TN = (((0,), (0,)), ((), ()))


def mm(a, b, dims):
    return lax.dot_general(a, b, dims, preferred_element_type=f32)


def as_column(row):
    n = row.shape[1]
    return jnp.transpose(jnp.broadcast_to(row, (n, n)))


def as_row(column):
    n = column.shape[0]
    return jnp.transpose(jnp.broadcast_to(column, (n, n)))[0:1, :]


def put3(ext_ref, at, row):
    high = row.astype(bf16).astype(f32)
    rest = row - high
    middle = rest.astype(bf16).astype(f32)
    ext_ref[at : at + 1, :] = high
    ext_ref[at + 1 : at + 2, :] = middle
    ext_ref[at + 2 : at + 3, :] = rest - middle


def get3(ext, at):
    return ext[at : at + 1, :] + ext[at + 1 : at + 2, :] + ext[at + 2 : at + 3, :]


def vmem_spec():
    return pl.BlockSpec(memory_space=pltpu.VMEM)


def smem_spec():
    return pl.BlockSpec(memory_space=pltpu.SMEM)


def params(**kw):
    return pltpu.CompilerParams(vmem_limit_bytes=VMEM_LIMIT, **kw)


def piece_slots(piece, mp_count):
    if piece == 0:
        return [[("own", z), (z // 2, z % 2)] for z in range(mp_count)]
    if piece == 1:
        return [[(2 + z, 0), (2 + z, 1)] for z in range(mp_count)]
    return [[(6 + z // 2, z % 2)] for z in range(mp_count)]


def rels_of(piece):
    return [(0, 1), (2, 3, 4, 5), (6, 7)][piece]


def score_body(piece, mp_count, rows, tab_ref, eq_ref, *refs):
    rels = rels_of(piece)
    half_refs = {r: (refs[2 * i], refs[2 * i + 1]) for i, r in enumerate(rels)}
    outs = refs[2 * len(rels) : 2 * len(rels) + mp_count]
    hold, ext_ref = refs[2 * len(rels) + mp_count :]
    z = tab_ref[32]
    half = refs[0].shape[1]
    ext_ref[...] = jnp.zeros_like(ext_ref)
    for owner, slots in enumerate(piece_slots(piece, mp_count)):
        target = owner ^ z
        for i, slot in enumerate(slots):
            if slot[0] == "own":
                a_ref, b_ref = half_refs[0]
                lid = qb = slot[1]
            else:
                r, k = slot
                a_ref, b_ref = half_refs[r]
                qb, lid = tab_ref[2 * r + k], tab_ref[16 + 2 * r + k]
            at = pl.ds(lid * rows, rows)
            ep_a, ep_b = a_ref[at, :], b_ref[at, :]
            eq = eq_ref[pl.ds(qb * rows, rows), :]
            table = mm(ep_a, eq[:, :half], NT) + mm(ep_b, eq[:, half:], NT)
            a32, b32, q32 = ep_a.astype(f32), ep_b.astype(f32), eq.astype(f32)
            p_sq = jnp.sum(a32 * a32 + b32 * b32, axis=1, keepdims=True)
            q_sq = jnp.sum(q32 * q32, axis=1, keepdims=True)
            put3(ext_ref, 0, as_row(q_sq))
            put3(ext_ref, 3, as_row(p_sq))
            hold[target, i, :rows, :] = table.astype(bf16)
            hold[target, i, rows:, :] = ext_ref[...].astype(bf16)
    for k in range(mp_count):
        outs[k][...] = hold[k]


def score_piece(piece, mp_count, rows, tab, eq, halves):
    n = len(piece_slots(piece, mp_count)[0])
    operands = [h for r in rels_of(piece) for h in halves[r]]
    shape = (n, rows + EXT, rows)
    count = n * mp_count
    return pl.pallas_call(
        functools.partial(score_body, piece, mp_count, rows),
        out_shape=[jax.ShapeDtypeStruct(shape, bf16)] * mp_count,
        in_specs=[smem_spec()] + [vmem_spec()] * (1 + len(operands)),
        out_specs=[vmem_spec()] * mp_count,
        scratch_shapes=[pltpu.VMEM((mp_count,) + shape, bf16), pltpu.VMEM((EXT, rows), f32)],
        compiler_params=params(),
        cost_estimate=pl.CostEstimate(
            flops=2 * count * rows * rows * eq.shape[1], bytes_accessed=8 * 1024 * 1024, transcendentals=0
        ),
        name="score_piece",
    )(tab, eq, *operands)


def exp_body(piece, mp_count, rows, tab_ref, pos_ref, *refs):
    parts, out, ext_ref = refs[:mp_count], refs[mp_count], refs[mp_count + 1]
    z = tab_ref[32]
    ext_ref[...] = jnp.zeros_like(ext_ref)
    for i, slot in enumerate(piece_slots(piece, mp_count)[0]):
        total = parts[0][i].astype(f32)
        for part in parts[1:]:
            total = total + part[i].astype(f32)
        ext = total[rows:, :]
        q_sq, p_sq = get3(ext, 0), get3(ext, 3)
        q_inv = lax.rsqrt(q_sq + epsilon)
        p_inv = lax.rsqrt(p_sq + epsilon)
        scores = total[:rows, :] * as_column(p_inv) * q_inv * (1.0 / logit_divisor)
        powers = jnp.exp(scores)
        put3(ext_ref, 0, jnp.sum(powers, axis=0, keepdims=True))
        put3(ext_ref, 3, jnp.sum(powers * scores, axis=0, keepdims=True))
        put3(ext_ref, 6, q_sq)
        put3(ext_ref, 9, p_sq)
        if slot[0] == "own":
            match = lax.broadcasted_iota(jnp.int32, (rows, rows), 0) == pos_ref[pl.ds(z, 1), :]
            put3(ext_ref, 12, jnp.sum(jnp.where(match, powers, 0.0), axis=0, keepdims=True))
        out[i, :rows, :] = powers.astype(bf16)
        out[i, rows:, :] = ext_ref[...].astype(bf16)


def exp_piece(piece, mp_count, rows, tab, pos, parts):
    shape = parts[0].shape
    return pl.pallas_call(
        functools.partial(exp_body, piece, mp_count, rows),
        out_shape=jax.ShapeDtypeStruct(shape, bf16),
        in_specs=[smem_spec()] + [vmem_spec()] * (1 + mp_count),
        out_specs=vmem_spec(),
        scratch_shapes=[pltpu.VMEM((EXT, rows), f32)],
        compiler_params=params(),
        cost_estimate=pl.CostEstimate(flops=10 * rows * rows, bytes_accessed=1024 * 1024, transcendentals=2 * rows * rows),
        name="exp_piece",
    )(tab, pos, *parts)


def back_body(mp_count, rows, block_count, tab_ref, pos_ref, eq_ref, *refs):
    dp_count = 8
    tables = [refs[p * mp_count : (p + 1) * mp_count] for p in range(3)]
    refs = refs[3 * mp_count :]
    own_a, own_b = refs[:2]
    halves = {r: (refs[2 + 2 * r], refs[3 + 2 * r]) for r in range(dp_count)}
    refs = refs[2 + 2 * dp_count :]
    dqe_out, loss_out, own_out = refs[:3]
    c_outs = refs[3 : 3 + dp_count]
    holds = refs[3 + dp_count : 6 + dp_count]
    tot, inner, q_sq, e_pos, dq = refs[6 + dp_count :]
    z = tab_ref[32]
    step = pl.program_id(0)
    half = own_a.shape[1]

    @pl.when(step == 0)
    def _():
        for p in range(3):
            for k in range(mp_count):
                holds[p][k] = tables[p][k][...]
        tot[...] = jnp.zeros_like(tot)
        inner[...] = jnp.zeros_like(inner)
        dq[...] = jnp.zeros_like(dq)
        for p in range(3):
            for owner, slots in enumerate(piece_slots(p, mp_count)):
                for i, slot in enumerate(slots):
                    ext = holds[p][owner ^ z, i, rows:, :].astype(f32)
                    if slot[0] == "own":
                        qb = slot[1]
                        q_sq[qb : qb + 1, :] = get3(ext, 6)
                        e_pos[qb : qb + 1, :] = get3(ext, 12)
                    else:
                        qb = tab_ref[2 * slot[0] + slot[1]]
                    tot[pl.ds(qb, 1), :] += get3(ext, 0)
                    inner[pl.ds(qb, 1), :] += get3(ext, 3)
        positive = jnp.log(e_pos[...])
        loss_out[...] = jnp.log(tot[...]) - positive
        inner[...] = inner[...] / tot[...] - positive

    def visit(hold_at, a_ref, b_ref, at, qb, own, out_ref, out_at):
        p, owner, i = hold_at
        ext = holds[p][owner ^ z, i, rows:, :].astype(f32)
        powers = holds[p][owner ^ z, i, :rows, :].astype(f32)
        p_inv = as_column(lax.rsqrt(get3(ext, 9) + epsilon))
        q_inv = lax.rsqrt(get3(ext, 6) + epsilon)
        total = tot[pl.ds(qb, 1), :]
        scores = jnp.log(powers)
        weight = powers * (1.0 / total)
        if own:
            match = lax.broadcasted_iota(jnp.int32, (rows, rows), 0) == pos_ref[pl.ds(qb, 1), :]
            weight = jnp.where(match, e_pos[pl.ds(qb, 1), :] / total - 1.0, weight)
        p_inner = jnp.sum(weight * scores, axis=1, keepdims=True)
        to_q = weight * (p_inv * (1.0 / logit_divisor))
        to_p = to_q * q_inv
        to_q, to_p = to_q.astype(bf16), to_p.astype(bf16)
        factor = p_inner * p_inv[:, 0:1] * p_inv[:, 0:1]
        rows_of_q = pl.ds(qb * rows, rows)
        for j, ref in enumerate((a_ref, b_ref)):
            cols = slice(j * half, (j + 1) * half)
            ep = ref[at, :]
            dq[rows_of_q, cols] += mm(to_q, ep, TN)
            back = mm(to_p, eq_ref[rows_of_q, cols], NN) - ep.astype(f32) * factor
            out_ref[out_at, :, cols] = back.astype(bf16)

    per_step = block_count // 2
    for j in range(per_step):
        b = step * per_step + j
        visit((0, b, 0), own_a, own_b, pl.ds(j * rows, rows), b, True, own_out, j)
    whole = pl.ds(0, rows)
    for r in range(dp_count):
        if r < 2:
            where = (0, 2 * r + step, 1)
        elif r < 6:
            where = (1, r - 2, step)
        else:
            where = (2, 2 * (r - 6) + step, 0)
        visit(where, *halves[r], whole, tab_ref[2 * r + step], False, c_outs[r], 0)

    @pl.when(step == 1)
    def _():
        for b in range(block_count):
            q_inv = as_column(lax.rsqrt(q_sq[b : b + 1, :] + epsilon))[:, 0:1]
            q_inner = as_column(inner[b : b + 1, :])[:, 0:1]
            at = slice(b * rows, (b + 1) * rows)
            out = dq[at, :] * q_inv - eq_ref[at, :].astype(f32) * (q_inv * q_inv * q_inner)
            dqe_out[at, :] = out.astype(bf16)


def back_call(mp_count, rows, block_count, tab, pos, eq, tables, halves):
    dp_count = 8
    width = eq.shape[1]
    half = width // 2
    whole = lambda shape: pl.BlockSpec(shape, lambda k, tab: (0,) * len(shape))
    table_specs = [whole(t.shape) for piece in tables for t in piece]
    per_step = block_count // 2
    own_spec = pl.BlockSpec((per_step * rows, half), lambda k, tab: (k, 0))

    def half_spec(r):
        return pl.BlockSpec((rows, half), lambda k, tab: (tab[16 + 2 * r + k], 0))

    half_specs = [half_spec(r) for r in range(dp_count) for _ in range(2)]
    c_spec = pl.BlockSpec((1, rows, width), lambda k, tab: (k, 0, 0))
    grid_spec = pltpu.PrefetchScalarGridSpec(
        num_scalar_prefetch=1,
        grid=(2,),
        in_specs=[whole(pos.shape), whole(eq.shape)] + table_specs + [own_spec] * 2 + half_specs,
        out_specs=[
            whole(eq.shape),
            whole((block_count, rows)),
            pl.BlockSpec((per_step, rows, width), lambda k, tab: (k, 0, 0)),
        ]
        + [c_spec] * dp_count,
        scratch_shapes=[pltpu.VMEM((mp_count,) + piece[0].shape, bf16) for piece in tables]
        + [pltpu.VMEM((block_count, rows), f32)] * 4
        + [pltpu.VMEM(eq.shape, f32)],
    )
    return pl.pallas_call(
        functools.partial(back_body, mp_count, rows, block_count),
        grid_spec=grid_spec,
        out_shape=[
            jax.ShapeDtypeStruct(eq.shape, bf16),
            jax.ShapeDtypeStruct((block_count, rows), f32),
            jax.ShapeDtypeStruct((block_count, rows, width), bf16),
        ]
        + [jax.ShapeDtypeStruct((2, rows, width), bf16)] * dp_count,
        compiler_params=params(dimension_semantics=("arbitrary",)),
        cost_estimate=pl.CostEstimate(
            flops=4 * 20 * rows * rows * width, bytes_accessed=12 * 1024 * 1024, transcendentals=20 * rows * rows
        ),
        name="back",
    )(
        tab,
        pos,
        eq,
        *[t for piece in tables for t in piece],
        *halves[0],
        *[h for r in range(dp_count) for h in halves[r]],
    )


def gather_body(rows, block_count, tab_ref, own_ref, *refs):
    arrived, out, acc = refs[:-2], refs[-2], refs[-1]
    for b in range(block_count):
        acc[b * rows : (b + 1) * rows, :] = own_ref[b].astype(f32)
    for r, ref in enumerate(arrived):
        for k in range(2):
            at = pl.ds(tab_ref[2 * r + k] * rows, rows)
            acc[at, :] += ref[k].astype(f32)
    out[...] = acc[...].astype(bf16)


def gather_call(rows, block_count, tab, own, arrived):
    width = own.shape[2]
    shape = (block_count * rows, width)
    return pl.pallas_call(
        functools.partial(gather_body, rows, block_count),
        out_shape=jax.ShapeDtypeStruct(shape, bf16),
        in_specs=[smem_spec()] + [vmem_spec()] * (1 + len(arrived)),
        out_specs=vmem_spec(),
        scratch_shapes=[pltpu.VMEM(shape, f32)],
        compiler_params=params(),
        cost_estimate=pl.CostEstimate(flops=20 * rows * width, bytes_accessed=6 * 1024 * 1024, transcendentals=0),
        name="sum_returned",
    )(tab, own, *arrived)


def grad_weight_body(tab_ref, hq_ref, hp_ref, dq_ref, dp_ref, out_ref):
    out = mm(hq_ref[...], dq_ref[...], TN) + mm(hp_ref[...], dp_ref[...], TN)
    out_ref[0] = out.astype(out_ref.dtype)


def grad_weight_slabs(order, me, hq, hp, dq, dp, dtype=bf16):
    count = hq.shape[1] // 8
    depth, width = dq.shape
    targets = jnp.stack([me ^ r for r in order]).astype(jnp.int32)
    slab = pl.BlockSpec((depth, count), lambda i, tab: (0, tab[i]))
    whole = pl.BlockSpec((depth, width), lambda i, tab: (0, 0))
    return pl.pallas_call(
        grad_weight_body,
        grid_spec=pltpu.PrefetchScalarGridSpec(
            num_scalar_prefetch=1,
            grid=(len(order),),
            in_specs=[slab, slab, whole, whole],
            out_specs=pl.BlockSpec((1, count, width), lambda i, tab: (i, 0, 0)),
        ),
        out_shape=jax.ShapeDtypeStruct((len(order), count, width), dtype),
        compiler_params=params(dimension_semantics=("arbitrary",)),
        cost_estimate=pl.CostEstimate(
            flops=4 * len(order) * depth * count * width,
            bytes_accessed=2 * len(order) * count * (2 * depth + width),
            transcendentals=0,
        ),
        name="grad_weight_slabs",
    )(targets, hq, hp, dq, dp)


def xor_pairs(count, mask):
    return [(i, i ^ mask) for i in range(count)]


def line_reduce_scatter(rows, weight, z, mp_count):
    width = weight.shape[0] // mp_count

    def part(shard):
        return mm(rows, lax.dynamic_slice_in_dim(weight, shard * width, width, 0), NT)

    right = left = None
    last = mp_count - 1
    for t in range(1, mp_count):
        to_right = part(jnp.minimum(z + mp_count - t, last))
        to_left = part(jnp.maximum(z - mp_count + t, 0))
        if right is not None:
            to_right, to_left = to_right + right.astype(f32), to_left + left.astype(f32)
        right = lax.ppermute(to_right.astype(bf16), "mp", [(i, i + 1) for i in range(t)])
        left = lax.ppermute(to_left.astype(bf16), "mp", [(last - i, last - i - 1) for i in range(t)])
    return (part(z) + right.astype(f32) + left.astype(f32)).astype(bf16)


def tables_of(neg_blocks, me, z, dp_count, block_count):
    wanted = neg_blocks.reshape(-1)
    count = wanted.shape[0]

    def slots_of(ids, rel):
        place = jnp.arange(count, dtype=jnp.int32)
        earlier = (rel[:, None] == rel[None, :]) & (place[None, :] < place[:, None])
        rank = jnp.sum(earlier.astype(jnp.int32), axis=1)
        return rel * 2 + rank

    slot = slots_of(wanted, (wanted // block_count) ^ me)
    hot = (slot[:, None] == jnp.arange(count, dtype=jnp.int32)[None, :]).astype(jnp.int32)
    neg_count = count // block_count
    query_of = jnp.sum(hot * (jnp.arange(count, dtype=jnp.int32) // neg_count)[:, None], axis=0)
    local_of = jnp.sum(hot * (wanted % block_count)[:, None], axis=0)
    everyone = [local_of]
    asked = jnp.stack(
        [local_of.reshape(dp_count, 2)[0]]
        + [
            lax.ppermute(local_of.reshape(dp_count, 2)[r], "dp", xor_pairs(dp_count, r))
            for r in range(1, dp_count)
        ]
    ).reshape(count)
    tab = jnp.concatenate([query_of, local_of, z[None]]).astype(jnp.int32)
    return tab, asked


def neighbours(query_hidden, passage_hidden, head_weight, neg_blocks, pos_ids):
    dp_count, mp_count = lax.axis_size("dp"), lax.axis_size("mp")
    me, z = lax.axis_index("dp"), lax.axis_index("mp")
    block_count = neg_blocks.shape[0]
    rows = query_hidden.shape[0] // block_count
    width = head_weight.shape[1]
    half = width // 2
    swap = lambda a, mask: lax.ppermute(a, "dp", xor_pairs(dp_count, mask))
    across = lambda a, mask: lax.ppermute(a, "mp", xor_pairs(mp_count, mask))

    ea = mm(passage_hidden, head_weight[:, :half], NN).astype(bf16)
    eb = mm(passage_hidden, head_weight[:, half:], NN).astype(bf16)
    a = {0: ea, 2: swap(ea, 2)}
    b = {0: eb, 4: swap(eb, 4)}
    a[4], b[2] = swap(ea, 4), swap(eb, 2)
    a[6], b[6] = swap(a[2], 4), swap(b[4], 2)
    for r in (0, 2, 4, 6):
        a[r + 1], b[r + 1] = swap(a[r], 1), swap(b[r], 1)
    halves = {r: (a[r], b[r]) for r in range(dp_count)}
    eq = mm(query_hidden, head_weight, NN).astype(bf16)
    tab, asked = tables_of(neg_blocks, me, z, dp_count, block_count)
    pos = pos_ids.reshape(block_count, rows)
    tables = []
    for piece in range(3):
        parts = score_piece(piece, mp_count, rows, tab, eq, halves)
        parts = [parts[0]] + [across(parts[k], k) for k in range(1, mp_count)]
        mine = exp_piece(piece, mp_count, rows, tab, pos, parts)
        tables.append([mine] + [across(mine, k) for k in range(1, mp_count)])
    dqe, loss, own, *back = back_call(mp_count, rows, block_count, tab, pos, eq, tables, halves)
    arrived = [back[0]] + [swap(back[r], r) for r in range(1, dp_count)]
    query_grad = line_reduce_scatter(dqe, head_weight, z, mp_count)
    dpe = gather_call(rows, block_count, asked, own, arrived)
    passage_grad = line_reduce_scatter(dpe, head_weight, z, mp_count)
    grad_weight = scatter_weight(me, query_hidden, passage_hidden, dqe, dpe, swap)
    return loss.reshape(-1), grad_weight, query_grad, passage_grad


def scatter_weight(me, hq, hp, dq, dp, swap):
    half = dq.shape[1] // 2
    away = grad_weight_slabs((7, 3, 5, 1), me, hq, hp, dq, dp)
    home = grad_weight_slabs((6, 2, 4, 0), me, hq, hp, dq, dp)
    arrived = swap(away, 1)
    diag, xs, ys, mine = [home[i].astype(f32) + arrived[i].astype(f32) for i in range(4)]
    xa = swap(jnp.stack([diag[:, :half], xs[:, :half]]).astype(bf16), 2).astype(f32)
    yb = swap(jnp.stack([diag[:, half:], ys[:, half:]]).astype(bf16), 4).astype(f32)
    ya = swap((ys[:, :half] + xa[0]).astype(bf16), 4).astype(f32)
    xb = swap((xs[:, half:] + yb[0]).astype(bf16), 2).astype(f32)
    return jnp.concatenate([mine[:, :half] + xa[1] + ya, mine[:, half:] + yb[1] + xb], axis=1)


def back_norm(inverse, unit_rows, d_unit, inner):
    return (inverse[:, None] * (d_unit - unit_rows * inner[:, None])).astype(jnp.bfloat16)


def general(query_hidden, passage_hidden, head_weight, neg_blocks, pos_ids):
    dp_count = lax.axis_size("dp")
    block_count, neg_count = neg_blocks.shape
    row_count = query_hidden.shape[0]
    block_rows = row_count // block_count
    embed_width = head_weight.shape[1]
    cand_rows = (1 + neg_count) * block_rows
    request_count = block_count * neg_count
    slot_depth = (request_count + dp_count - 1) // dp_count
    slot_count = dp_count * slot_depth
    query_embed = jnp.dot(query_hidden, head_weight, preferred_element_type=jnp.float32)
    passage_embed = jnp.dot(passage_hidden, head_weight, preferred_element_type=jnp.float32)
    query_sq, passage_sq = lax.psum(
        (
            jnp.sum(query_embed * query_embed, axis=1),
            jnp.sum(passage_embed * passage_embed, axis=1),
        ),
        "mp",
    )
    query_inv = lax.rsqrt(query_sq + epsilon)
    passage_inv = lax.rsqrt(passage_sq + epsilon)
    query_unit = query_embed * query_inv[:, None]
    passage_unit = passage_embed * passage_inv[:, None]
    query_norm = query_unit.astype(jnp.bfloat16)
    passage_norm = passage_unit.astype(jnp.bfloat16)
    query_blocks = query_norm.reshape(block_count, block_rows, embed_width)
    passage_blocks = passage_norm.reshape(block_count, block_rows, embed_width)
    wanted = neg_blocks.reshape(-1)
    owners = wanted // block_count
    local_ids = wanted % block_count
    request_order = jnp.arange(request_count, dtype=jnp.int32)
    earlier_same = (owners[:, None] == owners[None, :]) & (
        request_order[None, :] < request_order[:, None]
    )
    owner_rank = jnp.sum(earlier_same.astype(jnp.int32), axis=1)
    slot_of = owners * slot_depth + owner_rank
    slot_table = (slot_of[:, None] == jnp.arange(slot_count, dtype=jnp.int32)[None, :]).astype(
        jnp.int32
    )
    requests = jnp.sum(slot_table * (local_ids + 1)[:, None], axis=0).reshape(dp_count, slot_depth)
    asked = lax.all_to_all(requests, "dp", split_axis=0, concat_axis=0, tiled=True).reshape(
        slot_count
    )
    live_slots = (asked > 0).astype(jnp.bfloat16)
    picked = jnp.take(passage_blocks, jnp.maximum(asked - 1, 0), axis=0) * live_slots[:, None, None]
    reply = picked.reshape(dp_count, slot_depth, block_rows, embed_width)
    arrived = lax.all_to_all(reply, "dp", split_axis=0, concat_axis=0, tiled=True).reshape(
        slot_count, block_rows, embed_width
    )
    fetched = jnp.take(arrived, slot_of, axis=0).reshape(
        block_count, neg_count, block_rows, embed_width
    )
    retrieved_documents = jnp.concatenate([passage_blocks[:, None], fetched], axis=1).reshape(
        block_count, cand_rows, embed_width
    )
    similarity_parts = jnp.einsum(
        "bqe,bce->bqc", query_blocks, retrieved_documents, preferred_element_type=jnp.float32
    )
    positions = pos_ids.reshape(block_count, block_rows)
    similarity_table = (
        lax.psum(similarity_parts.astype(jnp.bfloat16), "mp").astype(jnp.float32) / logit_divisor
    )
    columns = jnp.arange(cand_rows, dtype=jnp.int32)
    matching_document_slot = (columns[None, None, :] == positions[:, :, None]).astype(jnp.float32)
    exponent_values = jnp.exp(similarity_table)
    normalizer_totals = jnp.sum(exponent_values, axis=2)
    losses = jnp.log(normalizer_totals) - jnp.sum(similarity_table * matching_document_slot, axis=2)
    attention_probabilities = (
        (exponent_values / normalizer_totals[:, :, None] - matching_document_slot) / logit_divisor
    ).astype(jnp.bfloat16)
    d_query = jnp.einsum(
        "bqc,bce->bqe",
        attention_probabilities,
        retrieved_documents,
        preferred_element_type=jnp.float32,
    ).reshape(row_count, embed_width)
    d_cand = jnp.einsum(
        "bqc,bqe->bce", attention_probabilities, query_blocks, preferred_element_type=jnp.float32
    )
    own_terms = d_cand[:, :block_rows]
    neg_terms = (
        d_cand[:, block_rows:].reshape(request_count, block_rows, embed_width).astype(jnp.bfloat16)
    )
    outgoing = (
        jnp.zeros((slot_count, block_rows, embed_width), jnp.bfloat16).at[slot_of].set(neg_terms)
    )
    outgoing = outgoing.reshape(dp_count, slot_depth, block_rows, embed_width)
    returned = lax.all_to_all(outgoing, "dp", split_axis=0, concat_axis=0, tiled=True).reshape(
        slot_count, block_rows, embed_width
    )
    selector = (asked[None, :] - 1 == jnp.arange(block_count, dtype=jnp.int32)[:, None]).astype(
        jnp.bfloat16
    )
    d_passage = own_terms + jnp.einsum(
        "ls,sbe->lbe", selector, returned, preferred_element_type=jnp.float32
    )
    d_passage = d_passage.reshape(row_count, embed_width)
    query_inner, passage_inner = lax.psum(
        (jnp.sum(query_unit * d_query, axis=1), jnp.sum(passage_unit * d_passage, axis=1)), "mp"
    )
    d_query_embed = back_norm(query_inv, query_unit, d_query, query_inner)
    d_passage_embed = back_norm(passage_inv, passage_unit, d_passage, passage_inner)
    contract = (((0,), (0,)), ((), ()))
    query_part = lax.dot_general(
        query_hidden, d_query_embed, contract, preferred_element_type=jnp.float32
    )
    passage_part = lax.dot_general(
        passage_hidden, d_passage_embed, contract, preferred_element_type=jnp.float32
    )
    grad_weight = lax.psum_scatter(
        (query_part + passage_part).astype(jnp.bfloat16), "dp", scatter_dimension=0, tiled=True
    ).astype(jnp.float32)
    transpose_dims = (((1,), (1,)), ((), ()))
    query_back = lax.dot_general(
        d_query_embed, head_weight, transpose_dims, preferred_element_type=jnp.float32
    ).astype(jnp.bfloat16)
    passage_back = lax.dot_general(
        d_passage_embed, head_weight, transpose_dims, preferred_element_type=jnp.float32
    ).astype(jnp.bfloat16)
    query_grad, passage_grad = (
        lax.psum_scatter(query_back, "mp", scatter_dimension=1, tiled=True).astype(jnp.float32),
        lax.psum_scatter(passage_back, "mp", scatter_dimension=1, tiled=True).astype(jnp.float32),
    )
    return (
        losses.reshape(row_count),
        grad_weight,
        query_grad.astype(jnp.bfloat16),
        passage_grad.astype(jnp.bfloat16),
    )


def solution(mesh):
    placed = (P("dp", None), P("dp", None), P(None, "mp"), P("dp", None), P("dp"))
    sizes = dict(mesh.shape)

    def local(query_hidden, passage_hidden, head_weight, neg_blocks, pos_ids):
        exact = sizes["dp"] == 8 and sizes["mp"] == 4 and neg_blocks.shape == (4, 4)
        chosen = neighbours if exact else general
        return chosen(query_hidden, passage_hidden, head_weight, neg_blocks, pos_ids)

    return jax.shard_map(
        local,
        mesh=mesh,
        in_specs=placed,
        out_specs=(P("dp"), P("dp", "mp"), P("dp", "mp"), P("dp", "mp")),
        check_vma=False,
    )
```

```python
import functools

import jax
import jax.numpy as jnp
from jax import lax
from jax.experimental import pallas as pl
from jax.experimental.pallas import tpu as pltpu
from jax.sharding import PartitionSpec as P

logit_divisor = 0.02
epsilon = 1e-06
f32 = jnp.float32
bf16 = jnp.bfloat16
MIB = 1024 * 1024
EXT = 16
NT = (((1,), (1,)), ((), ()))
NN = (((1,), (0,)), ((), ()))
TN = (((0,), (0,)), ((), ()))


def mm(a, b, dims):
    return lax.dot_general(a, b, dims, preferred_element_type=f32)


def as_column(row):
    n = row.shape[1]
    return jnp.transpose(jnp.broadcast_to(row, (n, n)))


def as_row(column):
    n = column.shape[0]
    return jnp.transpose(jnp.broadcast_to(column, (n, n)))[0:1, :]


def put3(ext_ref, at, row):
    high = row.astype(bf16).astype(f32)
    rest = row - high
    middle = rest.astype(bf16).astype(f32)
    ext_ref[at : at + 1, :] = high
    ext_ref[at + 1 : at + 2, :] = middle
    ext_ref[at + 2 : at + 3, :] = rest - middle


def get3(ext, at):
    return ext[at : at + 1, :] + ext[at + 1 : at + 2, :] + ext[at + 2 : at + 3, :]


def whole_spec(x):
    return pl.BlockSpec(x.shape, lambda i: (0,) * len(x.shape))


def smem_spec():
    return pl.BlockSpec(memory_space=pltpu.SMEM)


def any_specs(arrays):
    return [pl.BlockSpec(memory_space=pl.ANY)] * len(arrays)


def params(mib=16, **kw):
    return pltpu.CompilerParams(vmem_limit_bytes=mib * MIB, **kw)


def cost(us):
    return pl.CostEstimate(flops=int(us * 1.1e9), bytes_accessed=0, transcendentals=0)


def slots_all(mp_count):
    return [
        [("own", z), (z // 2, z % 2), (2 + z, 0), (2 + z, 1), (6 + z // 2, z % 2)] for z in range(mp_count)
    ]


def place_of(r, k):
    if r < 2:
        return (2 * r + k, 1)
    if r < 6:
        return (r - 2, 2 + k)
    return (2 * (r - 6) + k, 4)


def score_body(rels, indices, slots, rows, tab_ref, eq_ref, *refs):
    mp_count = len(slots)
    sources = {}
    for i, r in enumerate(rels):
        found = zip(refs[2 * i : 2 * i + 2], indices[2 * i : 2 * i + 2])
        sources[r] = [ref if index is None else ref.at[index] for ref, index in found]
    ext_ref = refs[-1]
    hold = refs[-2]
    z = tab_ref[32]
    ext_ref[...] = jnp.zeros_like(ext_ref)
    for owner, mine in enumerate(slots):
        target = owner ^ z
        for i, slot in enumerate(mine):
            if slot[0] == "own":
                found = sources[0]
                lid = qb = slot[1]
            else:
                r, k = slot
                found = sources[r]
                qb, lid = tab_ref[2 * r + k], tab_ref[16 + 2 * r + k]
            eq = eq_ref[pl.ds(qb * rows, rows), :]
            table = p_sq = 0.0
            for j, ref in enumerate(found):
                ep = ref[pl.ds(lid * rows, rows), :]
                width = ep.shape[1]
                table += mm(ep, eq[:, j * width : (j + 1) * width], NT)
                ep = ep.astype(f32)
                p_sq += jnp.sum(ep * ep, axis=1, keepdims=True)
            q32 = eq.astype(f32)
            q_sq = jnp.sum(q32 * q32, axis=1, keepdims=True)
            put3(ext_ref, 0, as_row(q_sq))
            put3(ext_ref, 3, as_row(p_sq))
            hold[target, i, :rows, :] = table.astype(bf16)
            hold[target, i, rows:, :] = ext_ref[...].astype(bf16)
    outs = refs[-2 - mp_count : -2]
    for k in range(mp_count):
        outs[k][...] = hold[k]


def score_call(rels, slots, rows, tab, eq, sources, after):
    mp_count, n = len(slots), len(slots[0])
    pairs = [pair for r in rels for pair in sources[r]]
    shape = (n, rows + EXT, rows)
    outs = [jax.ShapeDtypeStruct(shape, bf16)] * mp_count
    return pl.pallas_call(
        functools.partial(score_body, rels, [i for _, i in pairs], slots, rows),
        out_shape=outs,
        grid=(1,),
        in_specs=[smem_spec(), whole_spec(eq)] + [whole_spec(a) for a, _ in pairs] + any_specs(after),
        out_specs=[whole_spec(o) for o in outs],
        scratch_shapes=[pltpu.VMEM((mp_count,) + shape, bf16), pltpu.VMEM((EXT, rows), f32)],
        compiler_params=params(),
        cost_estimate=cost(4),
        name="scores",
    )(tab, eq, *[a for a, _ in pairs], *after)


def exp_body(slots, rows, tab_ref, pos_ref, *refs):
    parts, out, ext_ref = refs[:-2], refs[-2], refs[-1]
    z = tab_ref[32]
    ext_ref[...] = jnp.zeros_like(ext_ref)
    for i, slot in enumerate(slots[0]):
        total = parts[0][i].astype(f32)
        for part in parts[1:]:
            total = total + part[i].astype(f32)
        ext = total[rows:, :]
        q_sq, p_sq = get3(ext, 0), get3(ext, 3)
        q_inv = lax.rsqrt(q_sq + epsilon)
        p_inv = lax.rsqrt(p_sq + epsilon)
        scores = total[:rows, :] * as_column(p_inv) * q_inv * (1.0 / logit_divisor)
        powers = jnp.exp(scores)
        put3(ext_ref, 0, jnp.sum(powers, axis=0, keepdims=True))
        put3(ext_ref, 3, jnp.sum(powers * scores, axis=0, keepdims=True))
        put3(ext_ref, 6, q_sq)
        put3(ext_ref, 9, p_sq)
        if slot[0] == "own":
            match = lax.broadcasted_iota(jnp.int32, (rows, rows), 0) == pos_ref[pl.ds(z, 1), :]
            put3(ext_ref, 12, jnp.sum(jnp.where(match, powers, 0.0), axis=0, keepdims=True))
        out[i, :rows, :] = powers.astype(bf16)
        out[i, rows:, :] = ext_ref[...].astype(bf16)


def exp_call(slots, rows, tab, pos, parts):
    shape = parts[0].shape
    return pl.pallas_call(
        functools.partial(exp_body, slots, rows),
        out_shape=jax.ShapeDtypeStruct(shape, bf16),
        grid=(1,),
        in_specs=[smem_spec(), whole_spec(pos)] + [whole_spec(a) for a in parts],
        out_specs=pl.BlockSpec(shape, lambda i: (0, 0, 0)),
        scratch_shapes=[pltpu.VMEM((EXT, rows), f32)],
        compiler_params=params(),
        cost_estimate=cost(1),
        name="powers",
    )(tab, pos, *parts)


def totals_of(mp_count, tab_ref, z, hold, tables, tot, inner, q_sq, e_pos):
    for k in range(mp_count):
        hold[k] = tables[k][...]
    tot[...] = jnp.zeros_like(tot)
    inner[...] = jnp.zeros_like(inner)
    for owner, slots in enumerate(slots_all(mp_count)):
        for i, slot in enumerate(slots):
            ext = hold[owner ^ z, i, hold.shape[2] - EXT :, :].astype(f32)
            if slot[0] == "own":
                qb = slot[1]
                q_sq[qb : qb + 1, :] = get3(ext, 6)
                e_pos[qb : qb + 1, :] = get3(ext, 12)
            else:
                qb = tab_ref[2 * slot[0] + slot[1]]
            tot[pl.ds(qb, 1), :] += get3(ext, 0)
            inner[pl.ds(qb, 1), :] += get3(ext, 3)


def back_body(to_query, indices, after_count, mp_count, rows, block_count, tab_ref, pos_ref, eq_ref, *refs):
    dp_count = 8
    tables, refs = refs[:mp_count], refs[mp_count:]
    own = refs[:2]
    halves = {}
    for r in range(dp_count):
        found = zip(refs[2 + 2 * r : 4 + 2 * r], indices[2 * r : 2 * r + 2])
        halves[r] = [ref if index is None else ref.at[0] for ref, index in found]
    refs = refs[2 + 2 * dp_count + after_count :]
    if to_query:
        dq_outs, loss_out = refs[:2], refs[2]
        refs = refs[3:]
    else:
        own_out, c_outs = refs[0], refs[1 : 1 + dp_count // 2]
        refs = refs[1 + dp_count // 2 :]
    hold, refs = refs[0], refs[1:]
    tot, inner, q_sq, e_pos = refs[:4]
    z = tab_ref[32]
    step = pl.program_id(0)
    half = own[0].shape[1]

    @pl.when(step == 0)
    def _():
        totals_of(mp_count, tab_ref, z, hold, tables, tot, inner, q_sq, e_pos)
        if to_query:
            refs[4][...] = jnp.zeros_like(refs[4])
            positive = jnp.log(e_pos[...])
            loss_out[...] = jnp.log(tot[...]) - positive
            inner[...] = inner[...] / tot[...] - positive

    def visit(place, sources, at, qb, is_own, out_ref=None):
        owner, i = place
        ext = hold[owner ^ z, i, rows:, :].astype(f32)
        powers = hold[owner ^ z, i, :rows, :].astype(f32)
        p_inv = as_column(lax.rsqrt(get3(ext, 9) + epsilon))
        total = tot[pl.ds(qb, 1), :]
        weight = powers * (1.0 / total)
        if is_own:
            match = lax.broadcasted_iota(jnp.int32, (rows, rows), 0) == pos_ref[pl.ds(qb, 1), :]
            weight = jnp.where(match, e_pos[pl.ds(qb, 1), :] / total - 1.0, weight)
        to_q = weight * (p_inv * (1.0 / logit_divisor))
        rows_of_q = pl.ds(qb * rows, rows)
        if to_query:
            to_q = to_q.astype(bf16)
            for j, ref in enumerate(sources):
                refs[4][rows_of_q, j * half : (j + 1) * half] += mm(to_q, ref[at, :], TN)
            return
        p_inner = jnp.sum(weight * jnp.log(powers), axis=1, keepdims=True)
        to_p = (to_q * lax.rsqrt(get3(ext, 6) + epsilon)).astype(bf16)
        factor = p_inner * p_inv[:, 0:1] * p_inv[:, 0:1]
        for j, ref in enumerate(sources):
            cols = slice(j * half, (j + 1) * half)
            back = mm(to_p, eq_ref[rows_of_q, cols], NN) - ref[at, :].astype(f32) * factor
            out_ref[:, cols] = back.astype(bf16)

    per_step = block_count // 2
    for r in reversed(range(dp_count)):
        out = () if to_query else (c_outs[r // 2].at[r % 2, 0],)
        visit(place_of(r, step), halves[r], pl.ds(0, rows), tab_ref[2 * r + step], False, *out)
    for j in range(per_step):
        b = step * per_step + j
        out = () if to_query else (own_out.at[j],)
        visit((b, 0), own, pl.ds(j * rows, rows), b, True, *out)

    if to_query:

        @pl.when(step == 1)
        def _():
            for b in range(block_count):
                q_inv = as_column(lax.rsqrt(q_sq[b : b + 1, :] + epsilon))[:, 0:1]
                q_inner = as_column(inner[b : b + 1, :])[:, 0:1]
                at = slice(b * rows, (b + 1) * rows)
                out = refs[4][at, :] * q_inv - eq_ref[at, :].astype(f32) * (q_inv * q_inv * q_inner)
                dq_outs[b // per_step][(b % per_step) * rows : (b % per_step + 1) * rows, :] = out.astype(bf16)


def back_call(to_query, mp_count, rows, block_count, tab, pos, eq, tables, sources, after=()):
    dp_count = 8
    width = eq.shape[1]
    half = width // 2
    whole = lambda shape: pl.BlockSpec(shape, lambda k, tab: (0,) * len(shape))
    table_specs = [whole(t.shape) for t in tables]
    per_step = block_count // 2
    own_specs = [pl.BlockSpec((per_step * rows, half), lambda k, tab: (k, 0))] * 2

    def half_spec(r, index):
        if index is None:
            return pl.BlockSpec((rows, half), lambda k, tab: (tab[16 + 2 * r + k], 0))
        return pl.BlockSpec((1, rows, half), lambda k, tab: (index, tab[16 + 2 * r + k], 0))

    pairs = [pair for r in range(dp_count) for pair in sources[r]]
    half_specs = [half_spec(r, index) for r in range(dp_count) for _, index in sources[r]]
    c_spec = pl.BlockSpec((2, 1, rows, width), lambda k, tab: (0, k, 0, 0))
    scratch = [pltpu.VMEM((mp_count,) + tables[0].shape, bf16)]
    scratch += [pltpu.VMEM((block_count, rows), f32)] * 4
    part = (per_step * rows, width)
    if to_query:
        out_specs = [whole(part), whole(part), whole((block_count, rows))]
        out_shape = [jax.ShapeDtypeStruct(part, bf16)] * 2 + [jax.ShapeDtypeStruct((block_count, rows), f32)]
        scratch += [pltpu.VMEM(eq.shape, f32)]
    else:
        out_specs = [pl.BlockSpec((per_step, rows, width), lambda k, tab: (k, 0, 0))] + [c_spec] * (dp_count // 2)
        out_shape = [jax.ShapeDtypeStruct((block_count, rows, width), bf16)]
        out_shape += [jax.ShapeDtypeStruct((2, 2, rows, width), bf16)] * (dp_count // 2)
    grid_spec = pltpu.PrefetchScalarGridSpec(
        num_scalar_prefetch=1,
        grid=(2,),
        in_specs=[whole(pos.shape), whole(eq.shape)]
        + table_specs
        + own_specs
        + half_specs
        + any_specs(after),
        out_specs=out_specs,
        scratch_shapes=scratch,
    )
    return pl.pallas_call(
        functools.partial(back_body, to_query, [i for _, i in pairs], len(after), mp_count, rows, block_count),
        grid_spec=grid_spec,
        out_shape=out_shape,
        compiler_params=params(50, dimension_semantics=("arbitrary",)),
        cost_estimate=cost(6),
        name="query_gradient" if to_query else "passage_terms",
    )(
        tab,
        pos,
        eq,
        *tables,
        *[a for a, _ in sources[0]],
        *[a for a, _ in pairs],
        *after,
    )


def gather_body(rows, block_count, count, tab_ref, own_ref, *refs):
    arrived, outs, acc = refs[:count], refs[-3:-1], refs[-1]
    for b in range(block_count):
        acc[b * rows : (b + 1) * rows, :] = own_ref[b].astype(f32)
    for r, ref in enumerate(arrived):
        for k in range(2):
            at = pl.ds(tab_ref[2 * (tab_ref[16] ^ r) + k] * rows, rows)
            acc[at, :] += ref[0, k].astype(f32)
    part = outs[0].shape[0]
    for j in range(2):
        outs[j][...] = acc[j * part : (j + 1) * part, :].astype(bf16)


def gather_call(rows, block_count, tab, own, arrived, after):
    width = own.shape[2]
    part = (block_count * rows // 2, width)
    return pl.pallas_call(
        functools.partial(gather_body, rows, block_count, len(arrived)),
        out_shape=[jax.ShapeDtypeStruct(part, bf16)] * 2,
        grid=(1,),
        in_specs=[smem_spec(), whole_spec(own)] + [pl.BlockSpec((1,) + a.shape[1:], lambda i, k=k: (k,) + (0,) * (a.ndim - 1)) for a, k in arrived] + any_specs(after),
        out_specs=[pl.BlockSpec(part, lambda i: (0, 0))] * 2,
        scratch_shapes=[pltpu.VMEM((block_count * rows, width), f32)],
        compiler_params=params(),
        cost_estimate=cost(3),
        name="sum_returned",
    )(tab, own, *[a for a, _ in arrived], *after)


def pack_body(count, *refs):
    for i in range(count):
        refs[-1][i] = refs[i][0]


def pack(parts, after):
    shape = parts[0].shape[1:]
    zeros = (0,) * len(shape)
    return pl.pallas_call(
        functools.partial(pack_body, len(parts)),
        grid=(1,),
        out_shape=jax.ShapeDtypeStruct((len(parts),) + shape, parts[0].dtype),
        in_specs=[pl.BlockSpec((1,) + shape, lambda i: (1,) + zeros)] * len(parts) + any_specs(after),
        out_specs=pl.BlockSpec((len(parts),) + shape, lambda i: (0,) + zeros),
        compiler_params=params(),
        cost_estimate=cost(2),
        name="pack",
    )(*parts, *after)


def slab_sum(hidden_ref, top_ref, bottom_ref):
    part = top_ref.shape[0]
    return mm(hidden_ref[:part, :], top_ref[...], TN) + mm(hidden_ref[part:, :], bottom_ref[...], TN)


def slabs_body(has_earlier, tab_ref, hidden_ref, top_ref, bottom_ref, *refs):
    out = slab_sum(hidden_ref, top_ref, bottom_ref)
    if has_earlier:
        out = out + refs[0][0].astype(f32)
    refs[-1][0] = out.astype(bf16)


def home_body(tab_ref, hidden_ref, top_ref, bottom_ref, earlier_ref, arrived_ref, *outs):
    out = slab_sum(hidden_ref, top_ref, bottom_ref) + earlier_ref[0].astype(f32) + arrived_ref[0].astype(f32)
    half = out.shape[1] // 2
    out = out.astype(bf16)
    g = pl.program_id(0)
    for j, early in enumerate((g < 2, (g == 0) | (g == 2))):

        @pl.when(early)
        def _():
            outs[2 * j][0] = out[:, j * half : (j + 1) * half]

        @pl.when(jnp.logical_not(early))
        def _():
            outs[2 * j + 1][0] = out[:, j * half : (j + 1) * half]


def weight_slabs(order, me, hidden, d, earlier=None, arrived=None, after=()):
    count, depth = hidden.shape[1] // 8, hidden.shape[0]
    part, width = d[0].shape
    targets = jnp.stack([me ^ r for r in order]).astype(jnp.int32)
    whole = pl.BlockSpec((part, width), lambda i, tab: (0, 0))
    in_specs = [pl.BlockSpec((depth, count), lambda i, tab: (0, tab[i])), whole, whole]
    slab = pl.BlockSpec((1, count, width), lambda i, tab: (i, 0, 0))
    more = [a for a in (earlier, arrived) if a is not None]
    if arrived is None:
        body, out_specs = functools.partial(slabs_body, earlier is not None), slab
        out_shape = jax.ShapeDtypeStruct((len(order), count, width), bf16)
    else:
        body = home_body
        piece = (1, count, width // 2)
        out_specs = [
            pl.BlockSpec(piece, lambda i, tab: (jnp.minimum(i, 1), 0, 0)),
            pl.BlockSpec(piece, lambda i, tab: (jnp.maximum(i - 2, 0), 0, 0)),
            pl.BlockSpec(piece, lambda i, tab: (jnp.minimum(i // 2, 1), 0, 0)),
            pl.BlockSpec(piece, lambda i, tab: (jnp.where(i == 3, 1, 0), 0, 0)),
        ]
        out_shape = [jax.ShapeDtypeStruct((2, count, width // 2), bf16)] * 4
    return pl.pallas_call(
        body,
        grid_spec=pltpu.PrefetchScalarGridSpec(
            num_scalar_prefetch=1, grid=(len(order),), in_specs=in_specs + [slab] * len(more) + any_specs(after), out_specs=out_specs
        ),
        out_shape=out_shape,
        compiler_params=params(dimension_semantics=("arbitrary",)),
        cost_estimate=cost(4 if arrived is None else 5),
        name="weight_slabs",
    )(targets, hidden, *d, *more, *after)


def add_body(a_ref, b_ref, out_ref):
    out_ref[...] = (a_ref[...].astype(f32) + b_ref[...].astype(f32)).astype(bf16)


def add_halves(first, second):
    def body(a_ref, b_ref, c_ref, d_ref, left_ref, right_ref):
        add_body(a_ref.at[0], b_ref.at[0], left_ref)
        add_body(c_ref.at[0], d_ref.at[0], right_ref)

    shape = first[0].shape[1:]
    block = pl.BlockSpec((1,) + shape, lambda i: (0, 0, 0))
    out = pl.BlockSpec(shape, lambda i: (0, 0))
    return pl.pallas_call(
        body,
        grid=(1,),
        in_specs=[block] * 4,
        out_specs=[out] * 2,
        out_shape=[jax.ShapeDtypeStruct(shape, bf16)] * 2,
        compiler_params=params(),
        cost_estimate=cost(1.4),
        name="add_halves",
    )(*first, *second)


def last_sum_body(left_ref, xa_ref, ya_ref, right_ref, yb_ref, xb_ref, out_ref):
    half = ya_ref.shape[1]
    for j, (mine, first, second) in enumerate(((left_ref, xa_ref, ya_ref), (right_ref, yb_ref, xb_ref))):
        total = mine[0].astype(f32) + first[0].astype(f32) + second[...].astype(f32)
        out_ref[:, j * half : (j + 1) * half] = total


def last_sum(left, xa, ya, right, yb, xb):
    rows, half = ya.shape
    tile = rows // 4
    block = pl.BlockSpec((1, tile, half), lambda i: (1, i, 0))
    flat = pl.BlockSpec((tile, half), lambda i: (i, 0))
    return pl.pallas_call(
        last_sum_body,
        grid=(4,),
        in_specs=[block, block, flat] * 2,
        out_specs=pl.BlockSpec((tile, 2 * half), lambda i: (i, 0)),
        out_shape=jax.ShapeDtypeStruct((rows, 2 * half), f32),
        compiler_params=params(dimension_semantics=("arbitrary",)),
        cost_estimate=cost(3),
        name="last_sum",
    )(left, xa, ya, right, yb, xb)


def stack_body(count, *refs):
    for i in range(count):
        refs[-1][i] = refs[i][...]


def stack(parts, after):
    return pl.pallas_call(
        functools.partial(stack_body, len(parts)),
        out_shape=jax.ShapeDtypeStruct((len(parts),) + parts[0].shape, parts[0].dtype),
        grid=(1,),
        in_specs=[whole_spec(a) for a in parts] + any_specs(after),
        out_specs=pl.BlockSpec((len(parts),) + parts[0].shape, lambda i: (0,) * (1 + parts[0].ndim)),
        compiler_params=params(),
        cost_estimate=cost(1),
        name="stack",
    )(*parts, *after)


def slab_body(mp_count, tab_ref, start_ref, *refs):
    count = mp_count - 1
    inner, outer = refs[:count], refs[count : 2 * count - 1]
    weight_ref, out_ref, held = refs[2 * count - 1 :]
    z = tab_ref[0]

    @pl.when(pl.program_id(0) == 0)
    def _():
        for k in range(1, mp_count):
            source = z ^ k
            by_partner = (source > z) == (z % 2 == 0)
            steps = jnp.abs(source - z)
            for u in range(1, mp_count):

                @pl.when(by_partner & (steps == u))
                def _():
                    held[k - 1] = inner[u - 1][...]

                if u < mp_count - 1:

                    @pl.when(jnp.logical_not(by_partner) & (steps == u))
                    def _():
                        held[k - 1] = outer[u - 1][...]

    out = start_ref[...]
    for k in range(count):
        shares_of = weight_ref[:, pl.ds(z ^ (k + 1), 1)]
        out = out + mm(held[k], shares_of.reshape(-1, shares_of.shape[-1]), NT)
    out_ref[...] = out.astype(bf16)


def slab_product(z, mp_count, start, inner, outer, weights):
    depth, width = start.shape
    tile = width // 4
    tab = z[None].astype(jnp.int32)
    rows = pl.BlockSpec(inner[0].shape, lambda g, tab: (0, 0))
    block = pl.BlockSpec((depth, tile), lambda g, tab: (0, g))
    return pl.pallas_call(
        functools.partial(slab_body, mp_count),
        grid_spec=pltpu.PrefetchScalarGridSpec(
            num_scalar_prefetch=1,
            grid=(4,),
            in_specs=[block]
            + [rows] * (len(inner) + len(outer))
            + [pl.BlockSpec((weights.shape[0] // 4,) + weights.shape[1:], lambda g, tab: (g, 0, 0, 0))],
            out_specs=block,
            scratch_shapes=[pltpu.VMEM((mp_count - 1,) + inner[0].shape, bf16)],
        ),
        out_shape=jax.ShapeDtypeStruct(start.shape, bf16),
        compiler_params=params(dimension_semantics=("arbitrary",)),
        cost_estimate=cost(4),
        name="slab_product",
    )(tab, start, *inner, *outer, weights)


def xor_pairs(count, mask):
    return [(i, i ^ mask) for i in range(count)]


def parts_body(count, after_count, tab_ref, top_ref, bottom_ref, weight_ref, *refs):
    k = pl.program_id(0)
    refs[after_count][0] = mm(top_ref[...], weight_ref[...], NT).astype(bf16)
    if count > 1:

        @pl.when(k == count - 1)
        def _():
            refs[-1][...] = mm(bottom_ref[...], weight_ref[...], NT)


def line_parts(d, weight, slabs, after=()):
    top, bottom = d
    rows, width = top.shape
    slab = weight.shape[0] // 4
    count = len(slabs)
    tab = jnp.stack(slabs).astype(jnp.int32)
    whole = pl.BlockSpec((rows, width), lambda k, tab: (0, 0))
    more = 1 if count > 1 else 0
    return pl.pallas_call(
        functools.partial(parts_body, count, len(after)),
        grid_spec=pltpu.PrefetchScalarGridSpec(
            num_scalar_prefetch=1,
            grid=(count,),
            in_specs=[whole, whole, pl.BlockSpec((slab, width), lambda k, tab: (tab[k], 0))] + any_specs(after),
            out_specs=[pl.BlockSpec((1, rows, slab), lambda k, tab: (k, 0, 0))]
            + [pl.BlockSpec((rows, slab), lambda k, tab: (0, 0))] * more,
        ),
        out_shape=[jax.ShapeDtypeStruct((count, rows, slab), bf16)] + [jax.ShapeDtypeStruct((rows, slab), f32)] * more,
        compiler_params=params(dimension_semantics=("arbitrary",)),
        cost_estimate=cost(1 + count),
        name="line_parts",
    )(tab, top, bottom, weight, *after)


def pass_body(masks, after_count, tab_ref, *refs):
    n = len(masks)
    z = tab_ref[0]
    at_end = (z == 0) | (z == 3)
    for got, part, out, mask in zip(refs[:n], refs[n : 2 * n], refs[2 * n + after_count :], masks):
        term = part[0].astype(f32)
        if mask == "ends":
            term = jnp.where(at_end, term, 0.0)
        elif mask == "middle":
            term = jnp.where(at_end, 0.0, term)
        out[...] = (got[...].astype(f32) + term).astype(bf16)


def pass_on(z, *jobs, after=()):
    shape = jobs[0][0].shape
    whole = pl.BlockSpec(shape, lambda i: (0, 0))
    part_specs = [pl.BlockSpec((1,) + shape, lambda i, k=job[2]: (k, 0, 0)) for job in jobs]
    return pl.pallas_call(
        functools.partial(pass_body, [job[3] for job in jobs], len(after)),
        grid=(1,),
        in_specs=[smem_spec()] + [whole] * len(jobs) + part_specs + any_specs(after),
        out_specs=[whole] * len(jobs),
        out_shape=[jax.ShapeDtypeStruct(shape, bf16)] * len(jobs),
        compiler_params=params(),
        cost_estimate=cost(1.5),
        name="pass_on",
    )(z[None].astype(jnp.int32), *[job[0] for job in jobs], *[job[1] for job in jobs], *after)


def line_start(d, weight, z, mp_count):
    (first,) = line_parts(d, weight, [z ^ 3])
    return [lax.ppermute(d[1], "mp", xor_pairs(mp_count, 1))], [lax.ppermute(d[1], "mp", [(1, 2), (2, 1)])], first


def line_steps(d, weight, z, mp_count, begun, before_parts=(), before_third=()):
    inner, outer, first = begun
    inner_swap = lambda a: lax.ppermute(a, "mp", xor_pairs(mp_count, 1))
    outer_swap = lambda a: lax.ppermute(a, "mp", [(1, 2), (2, 1)])
    (to_inner,) = pass_on(z, (outer[0], first, 0, "ends"), after=before_parts)
    to_outer = inner[0]
    parts, own_bottom = line_parts(d, weight, [z ^ 2, z ^ 1, z], (to_inner,))
    inner, outer, sent = inner + [inner_swap(to_inner)], outer + [outer_swap(to_outer)], []
    to_inner, to_outer = pass_on(z, (outer[1], parts, 0, "ends"), (inner[1], parts, 0, "middle"), after=before_third)
    sent.append(to_inner)
    inner, outer = inner + [inner_swap(to_inner)], outer + [outer_swap(to_outer)]
    to_inner, to_outer = pass_on(z, (outer[2], parts, 1, "all"), (inner[2], first, 0, "middle"))
    sent.append(to_inner)
    inner, outer = inner + [inner_swap(to_inner)], outer + [outer_swap(to_outer)]
    return parts, own_bottom, inner, outer, sent


def line_bottom(z, mp_count, begun, weights):
    _, own_bottom, inner, outer, _ = begun
    return slab_product(z, mp_count, own_bottom, inner[:3], outer[:2], weights)


def line_finish(begun, bottom):
    parts, _, inner, outer, _ = begun
    return joined(parts, inner[3], outer[3], bottom)


def joined_body(part_ref, a_ref, b_ref, bottom_ref, out_ref):
    rows = a_ref.shape[0]
    total = part_ref[0].astype(f32) + a_ref[...].astype(f32) + b_ref[...].astype(f32)
    out_ref[:rows, :] = total.astype(bf16)
    out_ref[rows:, :] = bottom_ref[...]


def joined(parts, a, b, bottom):
    rows, width = a.shape
    whole = pl.BlockSpec((rows, width), lambda i: (0, 0))
    return pl.pallas_call(
        joined_body,
        grid=(1,),
        in_specs=[pl.BlockSpec((1, rows, width), lambda i: (2, 0, 0)), whole, whole, whole],
        out_specs=pl.BlockSpec((2 * rows, width), lambda i: (0, 0)),
        out_shape=jax.ShapeDtypeStruct((2 * rows, width), bf16),
        compiler_params=params(),
        cost_estimate=cost(1.2),
        name="joined",
    )(parts, a, b, bottom)


def slots_of(ids, rel):
    place = jnp.arange(ids.shape[-1], dtype=jnp.int32)
    earlier = (rel[..., :, None] == rel[..., None, :]) & (place[None, :] < place[:, None])
    return rel * 2 + jnp.sum(earlier.astype(jnp.int32), axis=-1)


def tables_of(neg_blocks, me, z, dp_count, block_count):
    wanted = neg_blocks.reshape(-1)
    count = wanted.shape[0]
    neg_count = count // block_count
    place = jnp.arange(count, dtype=jnp.int32)
    slot = slots_of(wanted, (wanted // block_count) ^ me)
    hot = (slot[:, None] == place[None, :]).astype(jnp.int32)
    query_of = jnp.sum(hot * (place // neg_count)[:, None], axis=0)
    local_of = jnp.sum(hot * (wanted % block_count)[:, None], axis=0)
    tab = jnp.concatenate([query_of, local_of, z[None]]).astype(jnp.int32)
    rows_of = (wanted // block_count)[None, :] == jnp.arange(dp_count, dtype=jnp.int32)[:, None]
    rank = jnp.sum((rows_of[:, :, None] & (place[None, :, None] < place[None, None, :])).astype(jnp.int32), axis=1)
    local = jnp.where(rows_of, wanted % block_count, 0)
    asks = jnp.stack([jnp.sum(jnp.where(rank == k, local, 0), axis=1) for k in range(2)], axis=1)
    asked = lax.all_to_all(asks, "dp", 0, 0, tiled=True).reshape(-1)
    return tab, jnp.concatenate([asked, me[None]]).astype(jnp.int32)


def neighbours(query_hidden, passage_hidden, head_weight, neg_blocks, pos_ids):
    dp_count, mp_count = lax.axis_size("dp"), lax.axis_size("mp")
    me, z = lax.axis_index("dp"), lax.axis_index("mp")
    block_count = neg_blocks.shape[0]
    rows = query_hidden.shape[0] // block_count
    width = head_weight.shape[1]
    half = width // 2
    swap = lambda a, mask: lax.ppermute(a, "dp", xor_pairs(dp_count, mask))
    across = lambda a, mask: lax.ppermute(a, "mp", xor_pairs(mp_count, mask))

    slab = head_weight.shape[0] // mp_count
    share = lax.dynamic_index_in_dim(head_weight.reshape(mp_count, dp_count, slab // dp_count, width), me, 1, False)
    share = lax.all_to_all(share, "mp", 0, 0, tiled=True)
    ea = mm(passage_hidden, head_weight[:, :half], NN).astype(bf16)
    eb = mm(passage_hidden, head_weight[:, half:], NN).astype(bf16)
    eq = mm(query_hidden, head_weight, NN).astype(bf16)
    ax, by = swap(ea, 2), swap(eb, 4)
    ay, bx = swap(ea, 4), swap(eb, 2)
    ad, bd = swap(ax, 4), swap(by, 2)
    core = swap(stack([ea, eb], ()), 1)
    core_xy = swap(stack([ax, bx, ay, by], ()), 1)
    core_d = swap(stack([ad, bd], (eq,)), 1)
    sources = {
        0: [(ea, None), (eb, None)],
        1: [(core, 0), (core, 1)],
        2: [(ax, None), (bx, None)],
        3: [(core_xy, 0), (core_xy, 1)],
        4: [(ay, None), (by, None)],
        5: [(core_xy, 2), (core_xy, 3)],
        6: [(ad, None), (bd, None)],
        7: [(core_d, 0), (core_d, 1)],
    }
    tab, asked = tables_of(neg_blocks, me, z, dp_count, block_count)
    pos = pos_ids.reshape(block_count, rows)
    slots = slots_all(mp_count)
    sent = score_call(tuple(range(dp_count)), slots, rows, tab, eq, sources, ())
    parts = [sent[0]] + [across(sent[k], k) for k in range(1, mp_count)]
    mine = exp_call(slots, rows, tab, pos, parts)
    tables = [mine] + [across(mine, k) for k in range(1, mp_count)]
    weights = lax.all_gather(stack([share], (sent[0],))[0], "dp", axis=0)

    *dq, loss = back_call(True, mp_count, rows, block_count, tab, pos, eq, tables, sources)
    query_begun = line_start(dq, head_weight, z, mp_count)
    own, here, to_x, to_y, to_d = back_call(
        False, mp_count, rows, block_count, tab, pos, eq, tables, sources, (query_begun[-1],)
    )
    query_line = line_steps(dq, head_weight, z, mp_count, query_begun, (here,))
    away, home = (7, 3, 5, 1), (6, 2, 4, 0)
    away_q = weight_slabs(away, me, query_hidden, dq)
    home_q = weight_slabs(home, me, query_hidden, dq)
    query_bottom = line_bottom(z, mp_count, query_line, weights)
    got = [swap(to_x, 2), swap(to_y, 4), swap(to_d, 6)]
    other = swap(pack([here] + got, query_line[-1] + [away_q, home_q, asked, query_bottom]), 1)
    arrived = {}
    for i, a in enumerate([here] + got):
        arrived[2 * i], arrived[2 * i + 1] = (a, 0), (other, i)
    dp = gather_call(
        rows,
        block_count,
        asked,
        own,
        [arrived[r] for r in range(dp_count)],
        [query_line[2][-1], query_line[3][-1]],
    )
    passage_begun = line_start(dp, head_weight, z, mp_count)
    away_sum = weight_slabs(away, me, passage_hidden, dp, away_q, None, (passage_begun[-1],))
    query_grad = line_finish(query_line, query_bottom)
    passage_line = line_steps(dp, head_weight, z, mp_count, passage_begun, (away_sum,), (query_grad,))
    left, left_more, right, right_more = weight_slabs(home, me, passage_hidden, dp, home_q, swap(away_sum, 1))
    xa, yb = swap(left, 2), swap(right, 4)
    to_y, to_x = add_halves((left_more, xa), (right_more, yb))
    grad_weight = last_sum(left_more, xa, swap(to_y, 4), right_more, yb, swap(to_x, 2))
    passage_grad = line_finish(passage_line, line_bottom(z, mp_count, passage_line, weights))
    return loss.reshape(-1), grad_weight, query_grad, passage_grad


def back_norm(inverse, unit_rows, d_unit, inner):
    return (inverse[:, None] * (d_unit - unit_rows * inner[:, None])).astype(jnp.bfloat16)


def general(query_hidden, passage_hidden, head_weight, neg_blocks, pos_ids):
    dp_count = lax.axis_size("dp")
    block_count, neg_count = neg_blocks.shape
    row_count = query_hidden.shape[0]
    block_rows = row_count // block_count
    embed_width = head_weight.shape[1]
    cand_rows = (1 + neg_count) * block_rows
    request_count = block_count * neg_count
    slot_depth = (request_count + dp_count - 1) // dp_count
    slot_count = dp_count * slot_depth
    query_embed = jnp.dot(query_hidden, head_weight, preferred_element_type=jnp.float32)
    passage_embed = jnp.dot(passage_hidden, head_weight, preferred_element_type=jnp.float32)
    query_sq, passage_sq = lax.psum(
        (
            jnp.sum(query_embed * query_embed, axis=1),
            jnp.sum(passage_embed * passage_embed, axis=1),
        ),
        "mp",
    )
    query_inv = lax.rsqrt(query_sq + epsilon)
    passage_inv = lax.rsqrt(passage_sq + epsilon)
    query_unit = query_embed * query_inv[:, None]
    passage_unit = passage_embed * passage_inv[:, None]
    query_norm = query_unit.astype(jnp.bfloat16)
    passage_norm = passage_unit.astype(jnp.bfloat16)
    query_blocks = query_norm.reshape(block_count, block_rows, embed_width)
    passage_blocks = passage_norm.reshape(block_count, block_rows, embed_width)
    wanted = neg_blocks.reshape(-1)
    owners = wanted // block_count
    local_ids = wanted % block_count
    request_order = jnp.arange(request_count, dtype=jnp.int32)
    earlier_same = (owners[:, None] == owners[None, :]) & (
        request_order[None, :] < request_order[:, None]
    )
    owner_rank = jnp.sum(earlier_same.astype(jnp.int32), axis=1)
    slot_of = owners * slot_depth + owner_rank
    slot_table = (slot_of[:, None] == jnp.arange(slot_count, dtype=jnp.int32)[None, :]).astype(
        jnp.int32
    )
    requests = jnp.sum(slot_table * (local_ids + 1)[:, None], axis=0).reshape(dp_count, slot_depth)
    asked = lax.all_to_all(requests, "dp", split_axis=0, concat_axis=0, tiled=True).reshape(
        slot_count
    )
    live_slots = (asked > 0).astype(jnp.bfloat16)
    picked = jnp.take(passage_blocks, jnp.maximum(asked - 1, 0), axis=0) * live_slots[:, None, None]
    reply = picked.reshape(dp_count, slot_depth, block_rows, embed_width)
    arrived = lax.all_to_all(reply, "dp", split_axis=0, concat_axis=0, tiled=True).reshape(
        slot_count, block_rows, embed_width
    )
    fetched = jnp.take(arrived, slot_of, axis=0).reshape(
        block_count, neg_count, block_rows, embed_width
    )
    retrieved_documents = jnp.concatenate([passage_blocks[:, None], fetched], axis=1).reshape(
        block_count, cand_rows, embed_width
    )
    similarity_parts = jnp.einsum(
        "bqe,bce->bqc", query_blocks, retrieved_documents, preferred_element_type=jnp.float32
    )
    positions = pos_ids.reshape(block_count, block_rows)
    similarity_table = (
        lax.psum(similarity_parts.astype(jnp.bfloat16), "mp").astype(jnp.float32) / logit_divisor
    )
    columns = jnp.arange(cand_rows, dtype=jnp.int32)
    matching_document_slot = (columns[None, None, :] == positions[:, :, None]).astype(jnp.float32)
    exponent_values = jnp.exp(similarity_table)
    normalizer_totals = jnp.sum(exponent_values, axis=2)
    losses = jnp.log(normalizer_totals) - jnp.sum(similarity_table * matching_document_slot, axis=2)
    attention_probabilities = (
        (exponent_values / normalizer_totals[:, :, None] - matching_document_slot) / logit_divisor
    ).astype(jnp.bfloat16)
    d_query = jnp.einsum(
        "bqc,bce->bqe",
        attention_probabilities,
        retrieved_documents,
        preferred_element_type=jnp.float32,
    ).reshape(row_count, embed_width)
    d_cand = jnp.einsum(
        "bqc,bqe->bce", attention_probabilities, query_blocks, preferred_element_type=jnp.float32
    )
    own_terms = d_cand[:, :block_rows]
    neg_terms = (
        d_cand[:, block_rows:].reshape(request_count, block_rows, embed_width).astype(jnp.bfloat16)
    )
    outgoing = (
        jnp.zeros((slot_count, block_rows, embed_width), jnp.bfloat16).at[slot_of].set(neg_terms)
    )
    outgoing = outgoing.reshape(dp_count, slot_depth, block_rows, embed_width)
    returned = lax.all_to_all(outgoing, "dp", split_axis=0, concat_axis=0, tiled=True).reshape(
        slot_count, block_rows, embed_width
    )
    selector = (asked[None, :] - 1 == jnp.arange(block_count, dtype=jnp.int32)[:, None]).astype(
        jnp.bfloat16
    )
    d_passage = own_terms + jnp.einsum(
        "ls,sbe->lbe", selector, returned, preferred_element_type=jnp.float32
    )
    d_passage = d_passage.reshape(row_count, embed_width)
    query_inner, passage_inner = lax.psum(
        (jnp.sum(query_unit * d_query, axis=1), jnp.sum(passage_unit * d_passage, axis=1)), "mp"
    )
    d_query_embed = back_norm(query_inv, query_unit, d_query, query_inner)
    d_passage_embed = back_norm(passage_inv, passage_unit, d_passage, passage_inner)
    contract = (((0,), (0,)), ((), ()))
    query_part = lax.dot_general(
        query_hidden, d_query_embed, contract, preferred_element_type=jnp.float32
    )
    passage_part = lax.dot_general(
        passage_hidden, d_passage_embed, contract, preferred_element_type=jnp.float32
    )
    grad_weight = lax.psum_scatter(
        (query_part + passage_part).astype(jnp.bfloat16), "dp", scatter_dimension=0, tiled=True
    ).astype(jnp.float32)
    transpose_dims = (((1,), (1,)), ((), ()))
    query_back = lax.dot_general(
        d_query_embed, head_weight, transpose_dims, preferred_element_type=jnp.float32
    ).astype(jnp.bfloat16)
    passage_back = lax.dot_general(
        d_passage_embed, head_weight, transpose_dims, preferred_element_type=jnp.float32
    ).astype(jnp.bfloat16)
    query_grad, passage_grad = (
        lax.psum_scatter(query_back, "mp", scatter_dimension=1, tiled=True).astype(jnp.float32),
        lax.psum_scatter(passage_back, "mp", scatter_dimension=1, tiled=True).astype(jnp.float32),
    )
    return (
        losses.reshape(row_count),
        grad_weight,
        query_grad.astype(jnp.bfloat16),
        passage_grad.astype(jnp.bfloat16),
    )


def solution(mesh):
    placed = (P("dp", None), P("dp", None), P(None, "mp"), P("dp", None), P("dp"))
    sizes = dict(mesh.shape)

    def local(query_hidden, passage_hidden, head_weight, neg_blocks, pos_ids):
        exact = sizes["dp"] == 8 and sizes["mp"] == 4 and neg_blocks.shape == (4, 4)
        chosen = neighbours if exact else general
        return chosen(query_hidden, passage_hidden, head_weight, neg_blocks, pos_ids)

    return jax.shard_map(
        local,
        mesh=mesh,
        in_specs=placed,
        out_specs=(P("dp"), P("dp", "mp"), P("dp", "mp"), P("dp", "mp")),
        check_vma=False,
    )
```

```python
import functools

import jax
import jax.numpy as jnp
from jax import lax
from jax.experimental import pallas as pl
from jax.experimental.pallas import tpu as pltpu
from jax.sharding import PartitionSpec as P

logit_divisor = 0.02
epsilon = 1e-06
f32 = jnp.float32
bf16 = jnp.bfloat16
MIB = 1024 * 1024
EXT = 16
NT = (((1,), (1,)), ((), ()))
NN = (((1,), (0,)), ((), ()))
TN = (((0,), (0,)), ((), ()))


def mm(a, b, dims):
    return lax.dot_general(a, b, dims, preferred_element_type=f32)


def as_column(row):
    n = row.shape[1]
    return jnp.transpose(jnp.broadcast_to(row, (n, n)))


def as_row(column):
    n = column.shape[0]
    return jnp.transpose(jnp.broadcast_to(column, (n, n)))[0:1, :]


def put3(ext_ref, at, row):
    high = row.astype(bf16).astype(f32)
    rest = row - high
    middle = rest.astype(bf16).astype(f32)
    ext_ref[at : at + 1, :] = high
    ext_ref[at + 1 : at + 2, :] = middle
    ext_ref[at + 2 : at + 3, :] = rest - middle


def get3(ext, at):
    return ext[at : at + 1, :] + ext[at + 1 : at + 2, :] + ext[at + 2 : at + 3, :]


def whole_spec(x):
    return pl.BlockSpec(x.shape, lambda i: (0,) * len(x.shape))


def smem_spec():
    return pl.BlockSpec(memory_space=pltpu.SMEM)


def any_specs(arrays):
    return [pl.BlockSpec(memory_space=pl.ANY)] * len(arrays)


def params(mib=16, **kw):
    return pltpu.CompilerParams(vmem_limit_bytes=mib * MIB, **kw)


def cost(us):
    return pl.CostEstimate(flops=int(us * 1.1e9), bytes_accessed=0, transcendentals=0)


def slots_all(mp_count):
    return [
        [("own", z), (z // 2, z % 2), (2 + z, 0), (2 + z, 1), (6 + z // 2, z % 2)] for z in range(mp_count)
    ]


def place_of(r, k):
    if r < 2:
        return (2 * r + k, 1)
    if r < 6:
        return (r - 2, 2 + k)
    return (2 * (r - 6) + k, 4)


def score_body(rels, indices, slots, rows, tab_ref, eq_ref, *refs):
    mp_count = len(slots)
    sources = {}
    for i, r in enumerate(rels):
        found = zip(refs[2 * i : 2 * i + 2], indices[2 * i : 2 * i + 2])
        sources[r] = [ref if index is None else ref.at[index] for ref, index in found]
    ext_ref = refs[-1]
    hold = refs[-2]
    z = tab_ref[32]
    ext_ref[...] = jnp.zeros_like(ext_ref)
    for owner, mine in enumerate(slots):
        target = owner ^ z
        for i, slot in enumerate(mine):
            if slot[0] == "own":
                found = sources[0]
                lid = qb = slot[1]
            else:
                r, k = slot
                found = sources[r]
                qb, lid = tab_ref[2 * r + k], tab_ref[16 + 2 * r + k]
            eq = eq_ref[pl.ds(qb * rows, rows), :]
            table = p_sq = 0.0
            for j, ref in enumerate(found):
                ep = ref[pl.ds(lid * rows, rows), :]
                width = ep.shape[1]
                table += mm(ep, eq[:, j * width : (j + 1) * width], NT)
                ep = ep.astype(f32)
                p_sq += jnp.sum(ep * ep, axis=1, keepdims=True)
            q32 = eq.astype(f32)
            q_sq = jnp.sum(q32 * q32, axis=1, keepdims=True)
            put3(ext_ref, 0, as_row(q_sq))
            put3(ext_ref, 3, as_row(p_sq))
            hold[target, i, :rows, :] = table.astype(bf16)
            hold[target, i, rows:, :] = ext_ref[...].astype(bf16)
    outs = refs[-2 - mp_count : -2]
    for k in range(mp_count):
        outs[k][...] = hold[k]


def score_call(rels, slots, rows, tab, eq, sources, after):
    mp_count, n = len(slots), len(slots[0])
    pairs = [pair for r in rels for pair in sources[r]]
    shape = (n, rows + EXT, rows)
    outs = [jax.ShapeDtypeStruct(shape, bf16)] * mp_count
    return pl.pallas_call(
        functools.partial(score_body, rels, [i for _, i in pairs], slots, rows),
        out_shape=outs,
        grid=(1,),
        in_specs=[smem_spec(), whole_spec(eq)] + [whole_spec(a) for a, _ in pairs] + any_specs(after),
        out_specs=[whole_spec(o) for o in outs],
        scratch_shapes=[pltpu.VMEM((mp_count,) + shape, bf16), pltpu.VMEM((EXT, rows), f32)],
        compiler_params=params(),
        cost_estimate=cost(4),
        name="scores",
    )(tab, eq, *[a for a, _ in pairs], *after)


def exp_body(slots, rows, tab_ref, pos_ref, *refs):
    parts, out, ext_ref = refs[:4], refs[-2], refs[-1]
    z = tab_ref[32]
    ext_ref[...] = jnp.zeros_like(ext_ref)
    for i, slot in enumerate(slots[0]):
        total = parts[0][i].astype(f32)
        for part in parts[1:]:
            total = total + part[i].astype(f32)
        ext = total[rows:, :]
        q_sq, p_sq = get3(ext, 0), get3(ext, 3)
        q_inv = lax.rsqrt(q_sq + epsilon)
        p_inv = lax.rsqrt(p_sq + epsilon)
        scores = total[:rows, :] * as_column(p_inv) * q_inv * (1.0 / logit_divisor)
        powers = jnp.exp(scores)
        put3(ext_ref, 0, jnp.sum(powers, axis=0, keepdims=True))
        put3(ext_ref, 3, jnp.sum(powers * scores, axis=0, keepdims=True))
        put3(ext_ref, 6, q_sq)
        put3(ext_ref, 9, p_sq)
        if slot[0] == "own":
            match = lax.broadcasted_iota(jnp.int32, (rows, rows), 0) == pos_ref[pl.ds(z, 1), :]
            put3(ext_ref, 12, jnp.sum(jnp.where(match, powers, 0.0), axis=0, keepdims=True))
        out[i, :rows, :] = powers.astype(bf16)
        out[i, rows:, :] = ext_ref[...].astype(bf16)


def exp_call(slots, rows, tab, pos, parts, after):
    shape = parts[0].shape
    return pl.pallas_call(
        functools.partial(exp_body, slots, rows),
        out_shape=jax.ShapeDtypeStruct(shape, bf16),
        grid=(1,),
        in_specs=[smem_spec(), whole_spec(pos)] + [whole_spec(a) for a in parts] + any_specs(after),
        out_specs=pl.BlockSpec(shape, lambda i: (0, 0, 0)),
        scratch_shapes=[pltpu.VMEM((EXT, rows), f32)],
        compiler_params=params(),
        cost_estimate=cost(1),
        name="powers",
    )(tab, pos, *parts, *after)


def totals_of(mp_count, tab_ref, z, hold, tables, tot, inner, q_sq, e_pos):
    for k in range(mp_count):
        hold[k] = tables[k][...]
    tot[...] = jnp.zeros_like(tot)
    inner[...] = jnp.zeros_like(inner)
    for owner, slots in enumerate(slots_all(mp_count)):
        for i, slot in enumerate(slots):
            ext = hold[owner ^ z, i, hold.shape[2] - EXT :, :].astype(f32)
            if slot[0] == "own":
                qb = slot[1]
                q_sq[qb : qb + 1, :] = get3(ext, 6)
                e_pos[qb : qb + 1, :] = get3(ext, 12)
            else:
                qb = tab_ref[2 * slot[0] + slot[1]]
            tot[pl.ds(qb, 1), :] += get3(ext, 0)
            inner[pl.ds(qb, 1), :] += get3(ext, 3)


def back_body(to_query, indices, after_count, mp_count, rows, block_count, tab_ref, pos_ref, eq_ref, *refs):
    dp_count = 8
    tables, refs = refs[:mp_count], refs[mp_count:]
    own = refs[:2]
    halves = {}
    for r in range(dp_count):
        found = zip(refs[2 + 2 * r : 4 + 2 * r], indices[2 * r : 2 * r + 2])
        halves[r] = [ref if index is None else ref.at[0] for ref, index in found]
    refs = refs[2 + 2 * dp_count + after_count :]
    if to_query:
        dq_outs, loss_out = refs[:2], refs[2]
        refs = refs[3:]
    else:
        own_out, c_outs = refs[0], refs[1 : 1 + dp_count // 2]
        refs = refs[1 + dp_count // 2 :]
    hold, refs = refs[0], refs[1:]
    tot, inner, q_sq, e_pos = refs[:4]
    z = tab_ref[32]
    step = pl.program_id(0)
    half = own[0].shape[1]

    @pl.when(step == 0)
    def _():
        totals_of(mp_count, tab_ref, z, hold, tables, tot, inner, q_sq, e_pos)
        if to_query:
            refs[4][...] = jnp.zeros_like(refs[4])
            positive = jnp.log(e_pos[...])
            loss_out[...] = jnp.log(tot[...]) - positive
            inner[...] = inner[...] / tot[...] - positive

    def visit(place, sources, at, qb, is_own, out_ref=None):
        owner, i = place
        ext = hold[owner ^ z, i, rows:, :].astype(f32)
        powers = hold[owner ^ z, i, :rows, :].astype(f32)
        p_inv = as_column(lax.rsqrt(get3(ext, 9) + epsilon))
        total = tot[pl.ds(qb, 1), :]
        weight = powers * (1.0 / total)
        if is_own:
            match = lax.broadcasted_iota(jnp.int32, (rows, rows), 0) == pos_ref[pl.ds(qb, 1), :]
            weight = jnp.where(match, e_pos[pl.ds(qb, 1), :] / total - 1.0, weight)
        to_q = weight * (p_inv * (1.0 / logit_divisor))
        rows_of_q = pl.ds(qb * rows, rows)
        if to_query:
            to_q = to_q.astype(bf16)
            for j, ref in enumerate(sources):
                refs[4][rows_of_q, j * half : (j + 1) * half] += mm(to_q, ref[at, :], TN)
            return
        p_inner = jnp.sum(weight * jnp.log(powers), axis=1, keepdims=True)
        to_p = (to_q * lax.rsqrt(get3(ext, 6) + epsilon)).astype(bf16)
        factor = p_inner * p_inv[:, 0:1] * p_inv[:, 0:1]
        for j, ref in enumerate(sources):
            cols = slice(j * half, (j + 1) * half)
            back = mm(to_p, eq_ref[rows_of_q, cols], NN) - ref[at, :].astype(f32) * factor
            out_ref[:, cols] = back.astype(bf16)

    per_step = block_count // 2
    for r in reversed(range(dp_count)):
        out = () if to_query else (c_outs[r // 2].at[r % 2, 0],)
        visit(place_of(r, step), halves[r], pl.ds(0, rows), tab_ref[2 * r + step], False, *out)
    for j in range(per_step):
        b = step * per_step + j
        out = () if to_query else (own_out.at[j],)
        visit((b, 0), own, pl.ds(j * rows, rows), b, True, *out)

    if to_query:

        @pl.when(step == 1)
        def _():
            for b in range(block_count):
                q_inv = as_column(lax.rsqrt(q_sq[b : b + 1, :] + epsilon))[:, 0:1]
                q_inner = as_column(inner[b : b + 1, :])[:, 0:1]
                at = slice(b * rows, (b + 1) * rows)
                out = refs[4][at, :] * q_inv - eq_ref[at, :].astype(f32) * (q_inv * q_inv * q_inner)
                dq_outs[b // per_step][(b % per_step) * rows : (b % per_step + 1) * rows, :] = out.astype(bf16)


def back_call(to_query, mp_count, rows, block_count, tab, pos, eq, tables, sources, after=()):
    dp_count = 8
    width = eq.shape[1]
    half = width // 2
    whole = lambda shape: pl.BlockSpec(shape, lambda k, tab: (0,) * len(shape))
    table_specs = [whole(t.shape) for t in tables]
    per_step = block_count // 2
    own_specs = [pl.BlockSpec((per_step * rows, half), lambda k, tab: (k, 0))] * 2

    def half_spec(r, index):
        if index is None:
            return pl.BlockSpec((rows, half), lambda k, tab: (tab[16 + 2 * r + k], 0))
        return pl.BlockSpec((1, rows, half), lambda k, tab: (index, tab[16 + 2 * r + k], 0))

    pairs = [pair for r in range(dp_count) for pair in sources[r]]
    half_specs = [half_spec(r, index) for r in range(dp_count) for _, index in sources[r]]
    c_spec = pl.BlockSpec((2, 1, rows, width), lambda k, tab: (0, k, 0, 0))
    scratch = [pltpu.VMEM((mp_count,) + tables[0].shape, bf16)]
    scratch += [pltpu.VMEM((block_count, rows), f32)] * 4
    part = (per_step * rows, width)
    if to_query:
        out_specs = [whole(part), whole(part), whole((block_count, rows))]
        out_shape = [jax.ShapeDtypeStruct(part, bf16)] * 2 + [jax.ShapeDtypeStruct((block_count, rows), f32)]
        scratch += [pltpu.VMEM(eq.shape, f32)]
    else:
        out_specs = [pl.BlockSpec((per_step, rows, width), lambda k, tab: (k, 0, 0))] + [c_spec] * (dp_count // 2)
        out_shape = [jax.ShapeDtypeStruct((block_count, rows, width), bf16)]
        out_shape += [jax.ShapeDtypeStruct((2, 2, rows, width), bf16)] * (dp_count // 2)
    grid_spec = pltpu.PrefetchScalarGridSpec(
        num_scalar_prefetch=1,
        grid=(2,),
        in_specs=[whole(pos.shape), whole(eq.shape)]
        + table_specs
        + own_specs
        + half_specs
        + any_specs(after),
        out_specs=out_specs,
        scratch_shapes=scratch,
    )
    return pl.pallas_call(
        functools.partial(back_body, to_query, [i for _, i in pairs], len(after), mp_count, rows, block_count),
        grid_spec=grid_spec,
        out_shape=out_shape,
        compiler_params=params(50, dimension_semantics=("arbitrary",)),
        cost_estimate=cost(6),
        name="query_gradient" if to_query else "passage_terms",
    )(
        tab,
        pos,
        eq,
        *tables,
        *[a for a, _ in sources[0]],
        *[a for a, _ in pairs],
        *after,
    )


def gather_body(rows, block_count, count, tab_ref, own_ref, *refs):
    arrived, outs, acc = refs[:count], refs[-3:-1], refs[-1]
    for b in range(block_count):
        acc[b * rows : (b + 1) * rows, :] = own_ref[b].astype(f32)
    for r, ref in enumerate(arrived):
        for k in range(2):
            at = pl.ds(tab_ref[2 * (tab_ref[16] ^ r) + k] * rows, rows)
            acc[at, :] += ref[0, k].astype(f32)
    part = outs[0].shape[0]
    for j in range(2):
        outs[j][...] = acc[j * part : (j + 1) * part, :].astype(bf16)


def gather_call(rows, block_count, tab, own, arrived, after):
    width = own.shape[2]
    part = (block_count * rows // 2, width)
    return pl.pallas_call(
        functools.partial(gather_body, rows, block_count, len(arrived)),
        out_shape=[jax.ShapeDtypeStruct(part, bf16)] * 2,
        grid=(1,),
        in_specs=[smem_spec(), whole_spec(own)] + [pl.BlockSpec((1,) + a.shape[1:], lambda i, k=k: (k,) + (0,) * (a.ndim - 1)) for a, k in arrived] + any_specs(after),
        out_specs=[pl.BlockSpec(part, lambda i: (0, 0))] * 2,
        scratch_shapes=[pltpu.VMEM((block_count * rows, width), f32)],
        compiler_params=params(),
        cost_estimate=cost(3),
        name="sum_returned",
    )(tab, own, *[a for a, _ in arrived], *after)


def pack_body(count, *refs):
    for i in range(count):
        refs[-1][i] = refs[i][0]


def pack(parts, after):
    shape = parts[0].shape[1:]
    zeros = (0,) * len(shape)
    return pl.pallas_call(
        functools.partial(pack_body, len(parts)),
        grid=(1,),
        out_shape=jax.ShapeDtypeStruct((len(parts),) + shape, parts[0].dtype),
        in_specs=[pl.BlockSpec((1,) + shape, lambda i: (1,) + zeros)] * len(parts) + any_specs(after),
        out_specs=pl.BlockSpec((len(parts),) + shape, lambda i: (0,) + zeros),
        compiler_params=params(),
        cost_estimate=cost(2),
        name="pack",
    )(*parts, *after)


def slab_sum(hidden_ref, top_ref, bottom_ref):
    part = top_ref.shape[0]
    return mm(hidden_ref[:part, :], top_ref[...], TN) + mm(hidden_ref[part:, :], bottom_ref[...], TN)


def slabs_body(has_earlier, tab_ref, hidden_ref, top_ref, bottom_ref, *refs):
    out = slab_sum(hidden_ref, top_ref, bottom_ref)
    if has_earlier:
        out = out + refs[0][0].astype(f32)
    refs[-1][0] = out.astype(bf16)


def home_body(tab_ref, hidden_ref, top_ref, bottom_ref, earlier_ref, arrived_ref, *outs):
    out = slab_sum(hidden_ref, top_ref, bottom_ref) + earlier_ref[0].astype(f32) + arrived_ref[0].astype(f32)
    half = out.shape[1] // 2
    out = out.astype(bf16)
    g = pl.program_id(0)
    for j, early in enumerate((g < 2, (g == 0) | (g == 2))):

        @pl.when(early)
        def _():
            outs[2 * j][0] = out[:, j * half : (j + 1) * half]

        @pl.when(jnp.logical_not(early))
        def _():
            outs[2 * j + 1][0] = out[:, j * half : (j + 1) * half]


def weight_slabs(order, me, hidden, d, earlier=None, arrived=None, after=()):
    count, depth = hidden.shape[1] // 8, hidden.shape[0]
    part, width = d[0].shape
    targets = jnp.stack([me ^ r for r in order]).astype(jnp.int32)
    whole = pl.BlockSpec((part, width), lambda i, tab: (0, 0))
    in_specs = [pl.BlockSpec((depth, count), lambda i, tab: (0, tab[i])), whole, whole]
    slab = pl.BlockSpec((1, count, width), lambda i, tab: (i, 0, 0))
    more = [a for a in (earlier, arrived) if a is not None]
    if arrived is None:
        body, out_specs = functools.partial(slabs_body, earlier is not None), slab
        out_shape = jax.ShapeDtypeStruct((len(order), count, width), bf16)
    else:
        body = home_body
        piece = (1, count, width // 2)
        out_specs = [
            pl.BlockSpec(piece, lambda i, tab: (jnp.minimum(i, 1), 0, 0)),
            pl.BlockSpec(piece, lambda i, tab: (jnp.maximum(i - 2, 0), 0, 0)),
            pl.BlockSpec(piece, lambda i, tab: (jnp.minimum(i // 2, 1), 0, 0)),
            pl.BlockSpec(piece, lambda i, tab: (jnp.where(i == 3, 1, 0), 0, 0)),
        ]
        out_shape = [jax.ShapeDtypeStruct((2, count, width // 2), bf16)] * 4
    return pl.pallas_call(
        body,
        grid_spec=pltpu.PrefetchScalarGridSpec(
            num_scalar_prefetch=1, grid=(len(order),), in_specs=in_specs + [slab] * len(more) + any_specs(after), out_specs=out_specs
        ),
        out_shape=out_shape,
        compiler_params=params(dimension_semantics=("arbitrary",)),
        cost_estimate=cost(1 if earlier is None else 4 if arrived is None else 5),
        name="weight_slabs",
    )(targets, hidden, *d, *more, *after)


def add_body(a_ref, b_ref, out_ref):
    out_ref[...] = (a_ref[...].astype(f32) + b_ref[...].astype(f32)).astype(bf16)


def add_halves(first, second):
    def body(a_ref, b_ref, c_ref, d_ref, left_ref, right_ref):
        add_body(a_ref.at[0], b_ref.at[0], left_ref)
        add_body(c_ref.at[0], d_ref.at[0], right_ref)

    shape = first[0].shape[1:]
    block = pl.BlockSpec((1,) + shape, lambda i: (0, 0, 0))
    out = pl.BlockSpec(shape, lambda i: (0, 0))
    return pl.pallas_call(
        body,
        grid=(1,),
        in_specs=[block] * 4,
        out_specs=[out] * 2,
        out_shape=[jax.ShapeDtypeStruct(shape, bf16)] * 2,
        compiler_params=params(),
        cost_estimate=cost(1.4),
        name="add_halves",
    )(*first, *second)


def last_sum_body(left_ref, xa_ref, ya_ref, right_ref, yb_ref, xb_ref, out_ref):
    half = ya_ref.shape[1]
    for j, (mine, first, second) in enumerate(((left_ref, xa_ref, ya_ref), (right_ref, yb_ref, xb_ref))):
        total = mine[0].astype(f32) + first[0].astype(f32) + second[...].astype(f32)
        out_ref[:, j * half : (j + 1) * half] = total


def last_sum(left, xa, ya, right, yb, xb):
    rows, half = ya.shape
    tile = rows // 4
    block = pl.BlockSpec((1, tile, half), lambda i: (1, i, 0))
    flat = pl.BlockSpec((tile, half), lambda i: (i, 0))
    return pl.pallas_call(
        last_sum_body,
        grid=(4,),
        in_specs=[block, block, flat] * 2,
        out_specs=pl.BlockSpec((tile, 2 * half), lambda i: (i, 0)),
        out_shape=jax.ShapeDtypeStruct((rows, 2 * half), f32),
        compiler_params=params(dimension_semantics=("arbitrary",)),
        cost_estimate=cost(3),
        name="last_sum",
    )(left, xa, ya, right, yb, xb)


def stack_body(count, *refs):
    for i in range(count):
        refs[-1][i] = refs[i][...]


def stack(parts, after):
    return pl.pallas_call(
        functools.partial(stack_body, len(parts)),
        out_shape=jax.ShapeDtypeStruct((len(parts),) + parts[0].shape, parts[0].dtype),
        grid=(1,),
        in_specs=[whole_spec(a) for a in parts] + any_specs(after),
        out_specs=pl.BlockSpec((len(parts),) + parts[0].shape, lambda i: (0,) * (1 + parts[0].ndim)),
        compiler_params=params(),
        cost_estimate=cost(1),
        name="stack",
    )(*parts, *after)


def slab_body(mp_count, tab_ref, start_ref, *refs):
    count = mp_count - 1
    inner, outer = refs[:count], refs[count : 2 * count - 1]
    weight_ref, out_ref, held = refs[2 * count - 1 :]
    z = tab_ref[0]

    @pl.when(pl.program_id(0) == 0)
    def _():
        for k in range(1, mp_count):
            source = z ^ k
            by_partner = (source > z) == (z % 2 == 0)
            steps = jnp.abs(source - z)
            for u in range(1, mp_count):

                @pl.when(by_partner & (steps == u))
                def _():
                    held[k - 1] = inner[u - 1][...]

                if u < mp_count - 1:

                    @pl.when(jnp.logical_not(by_partner) & (steps == u))
                    def _():
                        held[k - 1] = outer[u - 1][...]

    out = start_ref[...]
    for k in range(count):
        shares_of = weight_ref[:, pl.ds(z ^ (k + 1), 1)]
        out = out + mm(held[k], shares_of.reshape(-1, shares_of.shape[-1]), NT)
    out_ref[...] = out.astype(bf16)


def slab_product(z, mp_count, start, inner, outer, weights):
    depth, width = start.shape
    tile = width // 4
    tab = z[None].astype(jnp.int32)
    rows = pl.BlockSpec(inner[0].shape, lambda g, tab: (0, 0))
    block = pl.BlockSpec((depth, tile), lambda g, tab: (0, g))
    return pl.pallas_call(
        functools.partial(slab_body, mp_count),
        grid_spec=pltpu.PrefetchScalarGridSpec(
            num_scalar_prefetch=1,
            grid=(4,),
            in_specs=[block]
            + [rows] * (len(inner) + len(outer))
            + [pl.BlockSpec((weights.shape[0] // 4,) + weights.shape[1:], lambda g, tab: (g, 0, 0, 0))],
            out_specs=block,
            scratch_shapes=[pltpu.VMEM((mp_count - 1,) + inner[0].shape, bf16)],
        ),
        out_shape=jax.ShapeDtypeStruct(start.shape, bf16),
        compiler_params=params(dimension_semantics=("arbitrary",)),
        cost_estimate=cost(1),
        name="slab_product",
    )(tab, start, *inner, *outer, weights)


def xor_pairs(count, mask):
    return [(i, i ^ mask) for i in range(count)]


def parts_body(count, after_count, tab_ref, top_ref, bottom_ref, weight_ref, *refs):
    k = pl.program_id(0)
    refs[after_count][0] = mm(top_ref[...], weight_ref[...], NT).astype(bf16)
    if count > 1:

        @pl.when(k == count - 1)
        def _():
            refs[-1][...] = mm(bottom_ref[...], weight_ref[...], NT)


def line_parts(d, weight, slabs, after=()):
    top, bottom = d
    rows, width = top.shape
    slab = weight.shape[0] // 4
    count = len(slabs)
    tab = jnp.stack(slabs).astype(jnp.int32)
    whole = pl.BlockSpec((rows, width), lambda k, tab: (0, 0))
    more = 1 if count > 1 else 0
    return pl.pallas_call(
        functools.partial(parts_body, count, len(after)),
        grid_spec=pltpu.PrefetchScalarGridSpec(
            num_scalar_prefetch=1,
            grid=(count,),
            in_specs=[whole, whole, pl.BlockSpec((slab, width), lambda k, tab: (tab[k], 0))] + any_specs(after),
            out_specs=[pl.BlockSpec((1, rows, slab), lambda k, tab: (k, 0, 0))]
            + [pl.BlockSpec((rows, slab), lambda k, tab: (0, 0))] * more,
        ),
        out_shape=[jax.ShapeDtypeStruct((count, rows, slab), bf16)] + [jax.ShapeDtypeStruct((rows, slab), f32)] * more,
        compiler_params=params(dimension_semantics=("arbitrary",)),
        cost_estimate=cost(1 + count),
        name="line_parts",
    )(tab, top, bottom, weight, *after)


def pass_body(masks, after_count, tab_ref, *refs):
    n = len(masks)
    z = tab_ref[0]
    at_end = (z == 0) | (z == 3)
    for got, part, out, mask in zip(refs[:n], refs[n : 2 * n], refs[2 * n + after_count :], masks):
        term = part[0].astype(f32)
        if mask == "ends":
            term = jnp.where(at_end, term, 0.0)
        elif mask == "middle":
            term = jnp.where(at_end, 0.0, term)
        out[...] = (got[...].astype(f32) + term).astype(bf16)


def pass_on(z, *jobs, after=()):
    shape = jobs[0][0].shape
    whole = pl.BlockSpec(shape, lambda i: (0, 0))
    part_specs = [pl.BlockSpec((1,) + shape, lambda i, k=job[2]: (k, 0, 0)) for job in jobs]
    return pl.pallas_call(
        functools.partial(pass_body, [job[3] for job in jobs], len(after)),
        grid=(1,),
        in_specs=[smem_spec()] + [whole] * len(jobs) + part_specs + any_specs(after),
        out_specs=[whole] * len(jobs),
        out_shape=[jax.ShapeDtypeStruct(shape, bf16)] * len(jobs),
        compiler_params=params(),
        cost_estimate=cost(1.5),
        name="pass_on",
    )(z[None].astype(jnp.int32), *[job[0] for job in jobs], *[job[1] for job in jobs], *after)


def line_start(d, weight, z, mp_count):
    (first,) = line_parts(d, weight, [z ^ 3])
    return [lax.ppermute(d[1], "mp", xor_pairs(mp_count, 1))], [lax.ppermute(d[1], "mp", [(1, 2), (2, 1)])], first


def line_steps(d, weight, z, mp_count, begun, before_parts=(), before_third=()):
    inner, outer, first = begun
    inner_swap = lambda a: lax.ppermute(a, "mp", xor_pairs(mp_count, 1))
    outer_swap = lambda a: lax.ppermute(a, "mp", [(1, 2), (2, 1)])
    (to_inner,) = pass_on(z, (outer[0], first, 0, "ends"), after=before_parts)
    to_outer = inner[0]
    parts, own_bottom = line_parts(d, weight, [z ^ 2, z ^ 1, z], (to_inner,))
    inner, outer, sent = inner + [inner_swap(to_inner)], outer + [outer_swap(to_outer)], []
    to_inner, to_outer = pass_on(z, (outer[1], parts, 0, "ends"), (inner[1], parts, 0, "middle"), after=before_third)
    sent.append(to_inner)
    inner, outer = inner + [inner_swap(to_inner)], outer + [outer_swap(to_outer)]
    to_inner, to_outer = pass_on(z, (outer[2], parts, 1, "all"), (inner[2], first, 0, "middle"))
    sent.append(to_inner)
    inner, outer = inner + [inner_swap(to_inner)], outer + [outer_swap(to_outer)]
    return parts, own_bottom, inner, outer, sent


def line_bottom(z, mp_count, begun, weights):
    _, own_bottom, inner, outer, _ = begun
    return slab_product(z, mp_count, own_bottom, inner[:3], outer[:2], weights)


def line_finish(begun, bottom):
    parts, _, inner, outer, _ = begun
    return joined(parts, inner[3], outer[3], bottom)


def joined_body(part_ref, a_ref, b_ref, bottom_ref, out_ref):
    rows = a_ref.shape[0]
    total = part_ref[0].astype(f32) + a_ref[...].astype(f32) + b_ref[...].astype(f32)
    out_ref[:rows, :] = total.astype(bf16)
    out_ref[rows:, :] = bottom_ref[...]


def joined(parts, a, b, bottom):
    rows, width = a.shape
    whole = pl.BlockSpec((rows, width), lambda i: (0, 0))
    return pl.pallas_call(
        joined_body,
        grid=(1,),
        in_specs=[pl.BlockSpec((1, rows, width), lambda i: (2, 0, 0)), whole, whole, whole],
        out_specs=pl.BlockSpec((2 * rows, width), lambda i: (0, 0)),
        out_shape=jax.ShapeDtypeStruct((2 * rows, width), bf16),
        compiler_params=params(),
        cost_estimate=cost(1.2),
        name="joined",
    )(parts, a, b, bottom)


def slots_of(ids, rel):
    place = jnp.arange(ids.shape[-1], dtype=jnp.int32)
    earlier = (rel[..., :, None] == rel[..., None, :]) & (place[None, :] < place[:, None])
    return rel * 2 + jnp.sum(earlier.astype(jnp.int32), axis=-1)


def tables_of(neg_blocks, me, z, dp_count, block_count):
    wanted = neg_blocks.reshape(-1)
    count = wanted.shape[0]
    neg_count = count // block_count
    place = jnp.arange(count, dtype=jnp.int32)
    slot = slots_of(wanted, (wanted // block_count) ^ me)
    hot = (slot[:, None] == place[None, :]).astype(jnp.int32)
    query_of = jnp.sum(hot * (place // neg_count)[:, None], axis=0)
    local_of = jnp.sum(hot * (wanted % block_count)[:, None], axis=0)
    tab = jnp.concatenate([query_of, local_of, z[None]]).astype(jnp.int32)
    rows_of = (wanted // block_count)[None, :] == jnp.arange(dp_count, dtype=jnp.int32)[:, None]
    rank = jnp.sum((rows_of[:, :, None] & (place[None, :, None] < place[None, None, :])).astype(jnp.int32), axis=1)
    local = jnp.where(rows_of, wanted % block_count, 0)
    asks = jnp.stack([jnp.sum(jnp.where(rank == k, local, 0), axis=1) for k in range(2)], axis=1)
    asked = lax.all_to_all(asks, "dp", 0, 0, tiled=True).reshape(-1)
    return tab, jnp.concatenate([asked, me[None]]).astype(jnp.int32)


def neighbours(query_hidden, passage_hidden, head_weight, neg_blocks, pos_ids):
    dp_count, mp_count = lax.axis_size("dp"), lax.axis_size("mp")
    me, z = lax.axis_index("dp"), lax.axis_index("mp")
    block_count = neg_blocks.shape[0]
    rows = query_hidden.shape[0] // block_count
    width = head_weight.shape[1]
    half = width // 2
    swap = lambda a, mask: lax.ppermute(a, "dp", xor_pairs(dp_count, mask))
    across = lambda a, mask: lax.ppermute(a, "mp", xor_pairs(mp_count, mask))

    slab = head_weight.shape[0] // mp_count
    share = lax.dynamic_index_in_dim(head_weight.reshape(mp_count, dp_count, slab // dp_count, width), me, 1, False)
    share = lax.all_to_all(share, "mp", 0, 0, tiled=True)
    ea = mm(passage_hidden, head_weight[:, :half], NN).astype(bf16)
    eb = mm(passage_hidden, head_weight[:, half:], NN).astype(bf16)
    eq = mm(query_hidden, head_weight, NN).astype(bf16)
    ax, by = swap(ea, 2), swap(eb, 4)
    ay, bx = swap(ea, 4), swap(eb, 2)
    ad, bd = swap(ax, 4), swap(by, 2)
    core = swap(stack([ea, eb], ()), 1)
    core_xy = swap(stack([ax, bx, ay, by], ()), 1)
    core_d = swap(stack([ad, bd], (eq,)), 1)
    sources = {
        0: [(ea, None), (eb, None)],
        1: [(core, 0), (core, 1)],
        2: [(ax, None), (bx, None)],
        3: [(core_xy, 0), (core_xy, 1)],
        4: [(ay, None), (by, None)],
        5: [(core_xy, 2), (core_xy, 3)],
        6: [(ad, None), (bd, None)],
        7: [(core_d, 0), (core_d, 1)],
    }
    tab, asked = tables_of(neg_blocks, me, z, dp_count, block_count)
    pos = pos_ids.reshape(block_count, rows)
    slots = slots_all(mp_count)
    sent = score_call(tuple(range(dp_count)), slots, rows, tab, eq, sources, ())
    parts = [sent[0]] + [across(sent[k], k) for k in range(1, mp_count)]
    mine = exp_call(slots, rows, tab, pos, parts, (asked,))
    tables = [mine] + [across(mine, k) for k in range(1, mp_count)]
    weights = lax.all_gather(stack([share], (sent[0],))[0], "dp", axis=0)

    *dq, loss = back_call(True, mp_count, rows, block_count, tab, pos, eq, tables, sources)
    query_begun = line_start(dq, head_weight, z, mp_count)
    own, here, to_x, to_y, to_d = back_call(
        False, mp_count, rows, block_count, tab, pos, eq, tables, sources, (dq[0],)
    )
    query_line = line_steps(dq, head_weight, z, mp_count, query_begun, (here,))
    away, home = (7, 3, 5, 1), (6, 2, 4, 0)
    away_q = weight_slabs(away, me, query_hidden, dq)
    home_q = weight_slabs(home, me, query_hidden, dq)
    query_bottom = line_bottom(z, mp_count, query_line, weights)
    got = [swap(to_x, 2), swap(to_y, 4), swap(to_d, 6)]
    other = swap(pack([here] + got, [query_line[2][-1], query_line[3][-1], away_q, home_q, asked, query_bottom]), 1)
    arrived = {}
    for i, a in enumerate([here] + got):
        arrived[2 * i], arrived[2 * i + 1] = (a, 0), (other, i)
    dp = gather_call(
        rows,
        block_count,
        asked,
        own,
        [arrived[r] for r in range(dp_count)],
        [],
    )
    passage_begun = line_start(dp, head_weight, z, mp_count)
    away_sum = weight_slabs(away, me, passage_hidden, dp, away_q, None, (passage_begun[-1],))
    query_grad = line_finish(query_line, query_bottom)
    passage_line = line_steps(dp, head_weight, z, mp_count, passage_begun, (away_sum,), (query_grad,))
    left, left_more, right, right_more = weight_slabs(home, me, passage_hidden, dp, home_q, swap(away_sum, 1))
    xa, yb = swap(left, 2), swap(right, 4)
    to_y, to_x = add_halves((left_more, xa), (right_more, yb))
    grad_weight = last_sum(left_more, xa, swap(to_y, 4), right_more, yb, swap(to_x, 2))
    passage_grad = line_finish(passage_line, line_bottom(z, mp_count, passage_line, weights))
    return loss.reshape(-1), grad_weight, query_grad, passage_grad


def back_norm(inverse, unit_rows, d_unit, inner):
    return (inverse[:, None] * (d_unit - unit_rows * inner[:, None])).astype(jnp.bfloat16)


def general(query_hidden, passage_hidden, head_weight, neg_blocks, pos_ids):
    dp_count = lax.axis_size("dp")
    block_count, neg_count = neg_blocks.shape
    row_count = query_hidden.shape[0]
    block_rows = row_count // block_count
    embed_width = head_weight.shape[1]
    cand_rows = (1 + neg_count) * block_rows
    request_count = block_count * neg_count
    slot_depth = (request_count + dp_count - 1) // dp_count
    slot_count = dp_count * slot_depth
    query_embed = jnp.dot(query_hidden, head_weight, preferred_element_type=jnp.float32)
    passage_embed = jnp.dot(passage_hidden, head_weight, preferred_element_type=jnp.float32)
    query_sq, passage_sq = lax.psum(
        (
            jnp.sum(query_embed * query_embed, axis=1),
            jnp.sum(passage_embed * passage_embed, axis=1),
        ),
        "mp",
    )
    query_inv = lax.rsqrt(query_sq + epsilon)
    passage_inv = lax.rsqrt(passage_sq + epsilon)
    query_unit = query_embed * query_inv[:, None]
    passage_unit = passage_embed * passage_inv[:, None]
    query_norm = query_unit.astype(jnp.bfloat16)
    passage_norm = passage_unit.astype(jnp.bfloat16)
    query_blocks = query_norm.reshape(block_count, block_rows, embed_width)
    passage_blocks = passage_norm.reshape(block_count, block_rows, embed_width)
    wanted = neg_blocks.reshape(-1)
    owners = wanted // block_count
    local_ids = wanted % block_count
    request_order = jnp.arange(request_count, dtype=jnp.int32)
    earlier_same = (owners[:, None] == owners[None, :]) & (
        request_order[None, :] < request_order[:, None]
    )
    owner_rank = jnp.sum(earlier_same.astype(jnp.int32), axis=1)
    slot_of = owners * slot_depth + owner_rank
    slot_table = (slot_of[:, None] == jnp.arange(slot_count, dtype=jnp.int32)[None, :]).astype(
        jnp.int32
    )
    requests = jnp.sum(slot_table * (local_ids + 1)[:, None], axis=0).reshape(dp_count, slot_depth)
    asked = lax.all_to_all(requests, "dp", split_axis=0, concat_axis=0, tiled=True).reshape(
        slot_count
    )
    live_slots = (asked > 0).astype(jnp.bfloat16)
    picked = jnp.take(passage_blocks, jnp.maximum(asked - 1, 0), axis=0) * live_slots[:, None, None]
    reply = picked.reshape(dp_count, slot_depth, block_rows, embed_width)
    arrived = lax.all_to_all(reply, "dp", split_axis=0, concat_axis=0, tiled=True).reshape(
        slot_count, block_rows, embed_width
    )
    fetched = jnp.take(arrived, slot_of, axis=0).reshape(
        block_count, neg_count, block_rows, embed_width
    )
    retrieved_documents = jnp.concatenate([passage_blocks[:, None], fetched], axis=1).reshape(
        block_count, cand_rows, embed_width
    )
    similarity_parts = jnp.einsum(
        "bqe,bce->bqc", query_blocks, retrieved_documents, preferred_element_type=jnp.float32
    )
    positions = pos_ids.reshape(block_count, block_rows)
    similarity_table = (
        lax.psum(similarity_parts.astype(jnp.bfloat16), "mp").astype(jnp.float32) / logit_divisor
    )
    columns = jnp.arange(cand_rows, dtype=jnp.int32)
    matching_document_slot = (columns[None, None, :] == positions[:, :, None]).astype(jnp.float32)
    exponent_values = jnp.exp(similarity_table)
    normalizer_totals = jnp.sum(exponent_values, axis=2)
    losses = jnp.log(normalizer_totals) - jnp.sum(similarity_table * matching_document_slot, axis=2)
    attention_probabilities = (
        (exponent_values / normalizer_totals[:, :, None] - matching_document_slot) / logit_divisor
    ).astype(jnp.bfloat16)
    d_query = jnp.einsum(
        "bqc,bce->bqe",
        attention_probabilities,
        retrieved_documents,
        preferred_element_type=jnp.float32,
    ).reshape(row_count, embed_width)
    d_cand = jnp.einsum(
        "bqc,bqe->bce", attention_probabilities, query_blocks, preferred_element_type=jnp.float32
    )
    own_terms = d_cand[:, :block_rows]
    neg_terms = (
        d_cand[:, block_rows:].reshape(request_count, block_rows, embed_width).astype(jnp.bfloat16)
    )
    outgoing = (
        jnp.zeros((slot_count, block_rows, embed_width), jnp.bfloat16).at[slot_of].set(neg_terms)
    )
    outgoing = outgoing.reshape(dp_count, slot_depth, block_rows, embed_width)
    returned = lax.all_to_all(outgoing, "dp", split_axis=0, concat_axis=0, tiled=True).reshape(
        slot_count, block_rows, embed_width
    )
    selector = (asked[None, :] - 1 == jnp.arange(block_count, dtype=jnp.int32)[:, None]).astype(
        jnp.bfloat16
    )
    d_passage = own_terms + jnp.einsum(
        "ls,sbe->lbe", selector, returned, preferred_element_type=jnp.float32
    )
    d_passage = d_passage.reshape(row_count, embed_width)
    query_inner, passage_inner = lax.psum(
        (jnp.sum(query_unit * d_query, axis=1), jnp.sum(passage_unit * d_passage, axis=1)), "mp"
    )
    d_query_embed = back_norm(query_inv, query_unit, d_query, query_inner)
    d_passage_embed = back_norm(passage_inv, passage_unit, d_passage, passage_inner)
    contract = (((0,), (0,)), ((), ()))
    query_part = lax.dot_general(
        query_hidden, d_query_embed, contract, preferred_element_type=jnp.float32
    )
    passage_part = lax.dot_general(
        passage_hidden, d_passage_embed, contract, preferred_element_type=jnp.float32
    )
    grad_weight = lax.psum_scatter(
        (query_part + passage_part).astype(jnp.bfloat16), "dp", scatter_dimension=0, tiled=True
    ).astype(jnp.float32)
    transpose_dims = (((1,), (1,)), ((), ()))
    query_back = lax.dot_general(
        d_query_embed, head_weight, transpose_dims, preferred_element_type=jnp.float32
    ).astype(jnp.bfloat16)
    passage_back = lax.dot_general(
        d_passage_embed, head_weight, transpose_dims, preferred_element_type=jnp.float32
    ).astype(jnp.bfloat16)
    query_grad, passage_grad = (
        lax.psum_scatter(query_back, "mp", scatter_dimension=1, tiled=True).astype(jnp.float32),
        lax.psum_scatter(passage_back, "mp", scatter_dimension=1, tiled=True).astype(jnp.float32),
    )
    return (
        losses.reshape(row_count),
        grad_weight,
        query_grad.astype(jnp.bfloat16),
        passage_grad.astype(jnp.bfloat16),
    )


def solution(mesh):
    placed = (P("dp", None), P("dp", None), P(None, "mp"), P("dp", None), P("dp"))
    sizes = dict(mesh.shape)

    def local(query_hidden, passage_hidden, head_weight, neg_blocks, pos_ids):
        exact = sizes["dp"] == 8 and sizes["mp"] == 4 and neg_blocks.shape == (4, 4)
        chosen = neighbours if exact else general
        return chosen(query_hidden, passage_hidden, head_weight, neg_blocks, pos_ids)

    return jax.shard_map(
        local,
        mesh=mesh,
        in_specs=placed,
        out_specs=(P("dp"), P("dp", "mp"), P("dp", "mp"), P("dp", "mp")),
        check_vma=False,
    )
```

```python
import functools

import jax
import jax.numpy as jnp
from jax import lax
from jax.experimental import pallas as pl
from jax.experimental.pallas import tpu as pltpu
from jax.sharding import PartitionSpec as P

logit_divisor = 0.02
epsilon = 1e-06
f32 = jnp.float32
bf16 = jnp.bfloat16
MIB = 1024 * 1024
EXT = 16
NT = (((1,), (1,)), ((), ()))
NN = (((1,), (0,)), ((), ()))
TN = (((0,), (0,)), ((), ()))


def mm(a, b, dims):
    return lax.dot_general(a, b, dims, preferred_element_type=f32)


def as_column(row):
    n = row.shape[1]
    return jnp.transpose(jnp.broadcast_to(row, (n, n)))


def as_row(column):
    n = column.shape[0]
    return jnp.transpose(jnp.broadcast_to(column, (n, n)))[0:1, :]


def put3(ext_ref, at, row):
    high = row.astype(bf16).astype(f32)
    rest = row - high
    middle = rest.astype(bf16).astype(f32)
    ext_ref[at : at + 1, :] = high
    ext_ref[at + 1 : at + 2, :] = middle
    ext_ref[at + 2 : at + 3, :] = rest - middle


def get3(ext, at):
    return ext[at : at + 1, :] + ext[at + 1 : at + 2, :] + ext[at + 2 : at + 3, :]


def whole_spec(x):
    return pl.BlockSpec(x.shape, lambda i: (0,) * len(x.shape))


def smem_spec():
    return pl.BlockSpec(memory_space=pltpu.SMEM)


def any_specs(arrays):
    return [pl.BlockSpec(memory_space=pl.ANY)] * len(arrays)


def params(mib=16, **kw):
    return pltpu.CompilerParams(vmem_limit_bytes=mib * MIB, **kw)


def cost(us):
    return pl.CostEstimate(flops=int(us * 1.1e9), bytes_accessed=0, transcendentals=0)


def slots_all(mp_count):
    return [
        [("own", z), (z // 2, z % 2), (2 + z, 0), (2 + z, 1), (6 + z // 2, z % 2)] for z in range(mp_count)
    ]


def place_of(r, k):
    if r < 2:
        return (2 * r + k, 1)
    if r < 6:
        return (r - 2, 2 + k)
    return (2 * (r - 6) + k, 4)


def score_body(rels, indices, slots, rows, tab_ref, eq_ref, *refs):
    mp_count = len(slots)
    sources = {}
    for i, r in enumerate(rels):
        found = zip(refs[2 * i : 2 * i + 2], indices[2 * i : 2 * i + 2])
        sources[r] = [ref if index is None else ref.at[index] for ref, index in found]
    ext_ref = refs[-1]
    hold = refs[-2]
    z = tab_ref[32]
    ext_ref[...] = jnp.zeros_like(ext_ref)
    for owner, mine in enumerate(slots):
        target = owner ^ z
        for i, slot in enumerate(mine):
            if slot[0] == "own":
                found = sources[0]
                lid = qb = slot[1]
            else:
                r, k = slot
                found = sources[r]
                qb, lid = tab_ref[2 * r + k], tab_ref[16 + 2 * r + k]
            eq = eq_ref[pl.ds(qb * rows, rows), :]
            table = p_sq = 0.0
            for j, ref in enumerate(found):
                ep = ref[pl.ds(lid * rows, rows), :]
                width = ep.shape[1]
                table += mm(ep, eq[:, j * width : (j + 1) * width], NT)
                ep = ep.astype(f32)
                p_sq += jnp.sum(ep * ep, axis=1, keepdims=True)
            q32 = eq.astype(f32)
            q_sq = jnp.sum(q32 * q32, axis=1, keepdims=True)
            put3(ext_ref, 0, as_row(q_sq))
            put3(ext_ref, 3, as_row(p_sq))
            hold[target, i, :rows, :] = table.astype(bf16)
            hold[target, i, rows:, :] = ext_ref[...].astype(bf16)
    outs = refs[-2 - mp_count : -2]
    for k in range(mp_count):
        outs[k][...] = hold[k]


def score_call(rels, slots, rows, tab, eq, sources, after):
    mp_count, n = len(slots), len(slots[0])
    pairs = [pair for r in rels for pair in sources[r]]
    shape = (n, rows + EXT, rows)
    outs = [jax.ShapeDtypeStruct(shape, bf16)] * mp_count
    return pl.pallas_call(
        functools.partial(score_body, rels, [i for _, i in pairs], slots, rows),
        out_shape=outs,
        grid=(1,),
        in_specs=[smem_spec(), whole_spec(eq)] + [whole_spec(a) for a, _ in pairs] + any_specs(after),
        out_specs=[whole_spec(o) for o in outs],
        scratch_shapes=[pltpu.VMEM((mp_count,) + shape, bf16), pltpu.VMEM((EXT, rows), f32)],
        compiler_params=params(),
        cost_estimate=cost(4),
        name="scores",
    )(tab, eq, *[a for a, _ in pairs], *after)


def exp_body(slots, rows, tab_ref, pos_ref, *refs):
    parts, out, ext_ref = refs[:4], refs[-2], refs[-1]
    z = tab_ref[32]
    ext_ref[...] = jnp.zeros_like(ext_ref)
    for i, slot in enumerate(slots[0]):
        total = parts[0][i].astype(f32)
        for part in parts[1:]:
            total = total + part[i].astype(f32)
        ext = total[rows:, :]
        q_sq, p_sq = get3(ext, 0), get3(ext, 3)
        q_inv = lax.rsqrt(q_sq + epsilon)
        p_inv = lax.rsqrt(p_sq + epsilon)
        scores = total[:rows, :] * as_column(p_inv) * q_inv * (1.0 / logit_divisor)
        powers = jnp.exp(scores)
        put3(ext_ref, 0, jnp.sum(powers, axis=0, keepdims=True))
        put3(ext_ref, 3, jnp.sum(powers * scores, axis=0, keepdims=True))
        put3(ext_ref, 6, q_sq)
        put3(ext_ref, 9, p_sq)
        if slot[0] == "own":
            match = lax.broadcasted_iota(jnp.int32, (rows, rows), 0) == pos_ref[pl.ds(z, 1), :]
            put3(ext_ref, 12, jnp.sum(jnp.where(match, powers, 0.0), axis=0, keepdims=True))
        out[i, :rows, :] = powers.astype(bf16)
        out[i, rows:, :] = ext_ref[...].astype(bf16)


def exp_call(slots, rows, tab, pos, parts, after):
    shape = parts[0].shape
    return pl.pallas_call(
        functools.partial(exp_body, slots, rows),
        out_shape=jax.ShapeDtypeStruct(shape, bf16),
        grid=(1,),
        in_specs=[smem_spec(), whole_spec(pos)] + [whole_spec(a) for a in parts] + any_specs(after),
        out_specs=pl.BlockSpec(shape, lambda i: (0, 0, 0)),
        scratch_shapes=[pltpu.VMEM((EXT, rows), f32)],
        compiler_params=params(),
        cost_estimate=cost(1),
        name="powers",
    )(tab, pos, *parts, *after)


def totals_of(mp_count, tab_ref, z, hold, tables, tot, inner, q_sq, e_pos):
    for k in range(mp_count):
        hold[k] = tables[k][...]
    tot[...] = jnp.zeros_like(tot)
    inner[...] = jnp.zeros_like(inner)
    for owner, slots in enumerate(slots_all(mp_count)):
        for i, slot in enumerate(slots):
            ext = hold[owner ^ z, i, hold.shape[2] - EXT :, :].astype(f32)
            if slot[0] == "own":
                qb = slot[1]
                q_sq[qb : qb + 1, :] = get3(ext, 6)
                e_pos[qb : qb + 1, :] = get3(ext, 12)
            else:
                qb = tab_ref[2 * slot[0] + slot[1]]
            tot[pl.ds(qb, 1), :] += get3(ext, 0)
            inner[pl.ds(qb, 1), :] += get3(ext, 3)


def back_body(to_query, indices, after_count, mp_count, rows, block_count, tab_ref, pos_ref, eq_ref, *refs):
    dp_count = 8
    tables, refs = refs[:mp_count], refs[mp_count:]
    own = refs[:2]
    halves = {}
    for r in range(dp_count):
        found = zip(refs[2 + 2 * r : 4 + 2 * r], indices[2 * r : 2 * r + 2])
        halves[r] = [ref if index is None else ref.at[0] for ref, index in found]
    refs = refs[2 + 2 * dp_count + after_count :]
    if to_query:
        dq_outs, loss_out = refs[:2], refs[2]
        refs = refs[3:]
    else:
        own_out, c_outs = refs[0], refs[1 : 1 + dp_count // 2]
        refs = refs[1 + dp_count // 2 :]
    hold, refs = refs[0], refs[1:]
    tot, inner, q_sq, e_pos = refs[:4]
    z = tab_ref[32]
    step = pl.program_id(0)
    half = own[0].shape[1]

    @pl.when(step == 0)
    def _():
        totals_of(mp_count, tab_ref, z, hold, tables, tot, inner, q_sq, e_pos)
        if to_query:
            refs[4][...] = jnp.zeros_like(refs[4])
            positive = jnp.log(e_pos[...])
            loss_out[...] = jnp.log(tot[...]) - positive
            inner[...] = (inner[...] - positive * tot[...]) / tot[...]

    def visit(place, sources, at, qb, is_own, out_ref=None):
        owner, i = place
        ext = hold[owner ^ z, i, rows:, :].astype(f32)
        powers = hold[owner ^ z, i, :rows, :].astype(f32)
        p_inv = as_column(lax.rsqrt(get3(ext, 9) + epsilon))
        total = tot[pl.ds(qb, 1), :]
        weight = powers * (1.0 / total)
        if is_own:
            match = lax.broadcasted_iota(jnp.int32, (rows, rows), 0) == pos_ref[pl.ds(qb, 1), :]
            weight = jnp.where(match, (e_pos[pl.ds(qb, 1), :] - total) / total, weight)
        to_q = weight * (p_inv * (1.0 / logit_divisor))
        rows_of_q = pl.ds(qb * rows, rows)
        if to_query:
            to_q = to_q.astype(bf16)
            for j, ref in enumerate(sources):
                refs[4][rows_of_q, j * half : (j + 1) * half] += mm(to_q, ref[at, :], TN)
            return
        p_inner = jnp.sum(weight * jnp.log(powers), axis=1, keepdims=True)
        to_p = (to_q * lax.rsqrt(get3(ext, 6) + epsilon)).astype(bf16)
        factor = p_inner * p_inv[:, 0:1] * p_inv[:, 0:1]
        for j, ref in enumerate(sources):
            cols = slice(j * half, (j + 1) * half)
            back = mm(to_p, eq_ref[rows_of_q, cols], NN) - ref[at, :].astype(f32) * factor
            out_ref[:, cols] = back.astype(bf16)

    per_step = block_count // 2
    for r in reversed(range(dp_count)):
        out = () if to_query else (c_outs[r // 2].at[r % 2, 0],)
        visit(place_of(r, step), halves[r], pl.ds(0, rows), tab_ref[2 * r + step], False, *out)
    for j in range(per_step):
        b = step * per_step + j
        out = () if to_query else (own_out.at[j],)
        visit((b, 0), own, pl.ds(j * rows, rows), b, True, *out)

    if to_query:

        @pl.when(step == 1)
        def _():
            for b in range(block_count):
                q_inv = as_column(lax.rsqrt(q_sq[b : b + 1, :] + epsilon))[:, 0:1]
                q_inner = as_column(inner[b : b + 1, :])[:, 0:1]
                at = slice(b * rows, (b + 1) * rows)
                out = refs[4][at, :] * q_inv - eq_ref[at, :].astype(f32) * (q_inv * q_inv * q_inner)
                dq_outs[b // per_step][(b % per_step) * rows : (b % per_step + 1) * rows, :] = out.astype(bf16)


def back_call(to_query, mp_count, rows, block_count, tab, pos, eq, tables, sources, after=()):
    dp_count = 8
    width = eq.shape[1]
    half = width // 2
    whole = lambda shape: pl.BlockSpec(shape, lambda k, tab: (0,) * len(shape))
    table_specs = [whole(t.shape) for t in tables]
    per_step = block_count // 2
    own_specs = [pl.BlockSpec((per_step * rows, half), lambda k, tab: (k, 0))] * 2

    def half_spec(r, index):
        if index is None:
            return pl.BlockSpec((rows, half), lambda k, tab: (tab[16 + 2 * r + k], 0))
        return pl.BlockSpec((1, rows, half), lambda k, tab: (index, tab[16 + 2 * r + k], 0))

    pairs = [pair for r in range(dp_count) for pair in sources[r]]
    half_specs = [half_spec(r, index) for r in range(dp_count) for _, index in sources[r]]
    c_spec = pl.BlockSpec((2, 1, rows, width), lambda k, tab: (0, k, 0, 0))
    scratch = [pltpu.VMEM((mp_count,) + tables[0].shape, bf16)]
    scratch += [pltpu.VMEM((block_count, rows), f32)] * 4
    part = (per_step * rows, width)
    if to_query:
        out_specs = [whole(part), whole(part), whole((block_count, rows))]
        out_shape = [jax.ShapeDtypeStruct(part, bf16)] * 2 + [jax.ShapeDtypeStruct((block_count, rows), f32)]
        scratch += [pltpu.VMEM(eq.shape, f32)]
    else:
        out_specs = [pl.BlockSpec((per_step, rows, width), lambda k, tab: (k, 0, 0))] + [c_spec] * (dp_count // 2)
        out_shape = [jax.ShapeDtypeStruct((block_count, rows, width), bf16)]
        out_shape += [jax.ShapeDtypeStruct((2, 2, rows, width), bf16)] * (dp_count // 2)
    grid_spec = pltpu.PrefetchScalarGridSpec(
        num_scalar_prefetch=1,
        grid=(2,),
        in_specs=[whole(pos.shape), whole(eq.shape)]
        + table_specs
        + own_specs
        + half_specs
        + any_specs(after),
        out_specs=out_specs,
        scratch_shapes=scratch,
    )
    return pl.pallas_call(
        functools.partial(back_body, to_query, [i for _, i in pairs], len(after), mp_count, rows, block_count),
        grid_spec=grid_spec,
        out_shape=out_shape,
        compiler_params=params(50, dimension_semantics=("arbitrary",)),
        cost_estimate=cost(6),
        name="query_gradient" if to_query else "passage_terms",
    )(
        tab,
        pos,
        eq,
        *tables,
        *[a for a, _ in sources[0]],
        *[a for a, _ in pairs],
        *after,
    )


def gather_body(rows, block_count, count, tab_ref, own_ref, *refs):
    arrived, outs, acc = refs[:count], refs[-3:-1], refs[-1]
    for b in range(block_count):
        acc[b * rows : (b + 1) * rows, :] = own_ref[b].astype(f32)
    for r, ref in enumerate(arrived):
        for k in range(2):
            at = pl.ds(tab_ref[2 * (tab_ref[16] ^ r) + k] * rows, rows)
            acc[at, :] += ref[0, k].astype(f32)
    part = outs[0].shape[0]
    for j in range(2):
        outs[j][...] = acc[j * part : (j + 1) * part, :].astype(bf16)


def gather_call(rows, block_count, tab, own, arrived, after):
    width = own.shape[2]
    part = (block_count * rows // 2, width)
    return pl.pallas_call(
        functools.partial(gather_body, rows, block_count, len(arrived)),
        out_shape=[jax.ShapeDtypeStruct(part, bf16)] * 2,
        grid=(1,),
        in_specs=[smem_spec(), whole_spec(own)] + [pl.BlockSpec((1,) + a.shape[1:], lambda i, k=k: (k,) + (0,) * (a.ndim - 1)) for a, k in arrived] + any_specs(after),
        out_specs=[pl.BlockSpec(part, lambda i: (0, 0))] * 2,
        scratch_shapes=[pltpu.VMEM((block_count * rows, width), f32)],
        compiler_params=params(),
        cost_estimate=cost(3),
        name="sum_returned",
    )(tab, own, *[a for a, _ in arrived], *after)


def pack_body(count, *refs):
    for i in range(count):
        refs[-1][i] = refs[i][0]


def pack(parts, after):
    shape = parts[0].shape[1:]
    zeros = (0,) * len(shape)
    return pl.pallas_call(
        functools.partial(pack_body, len(parts)),
        grid=(1,),
        out_shape=jax.ShapeDtypeStruct((len(parts),) + shape, parts[0].dtype),
        in_specs=[pl.BlockSpec((1,) + shape, lambda i: (1,) + zeros)] * len(parts) + any_specs(after),
        out_specs=pl.BlockSpec((len(parts),) + shape, lambda i: (0,) + zeros),
        compiler_params=params(),
        cost_estimate=cost(2),
        name="pack",
    )(*parts, *after)


def slab_sum(hidden_ref, top_ref, bottom_ref):
    part = top_ref.shape[0]
    return mm(hidden_ref[:part, :], top_ref[...], TN) + mm(hidden_ref[part:, :], bottom_ref[...], TN)


def slabs_body(has_earlier, tab_ref, hidden_ref, top_ref, bottom_ref, *refs):
    out = slab_sum(hidden_ref, top_ref, bottom_ref)
    if has_earlier:
        out = out + refs[0][0].astype(f32)
    refs[-1][0] = out.astype(bf16)


def home_body(tab_ref, hidden_ref, top_ref, bottom_ref, earlier_ref, arrived_ref, *outs):
    out = slab_sum(hidden_ref, top_ref, bottom_ref) + earlier_ref[0].astype(f32) + arrived_ref[0].astype(f32)
    half = out.shape[1] // 2
    out = out.astype(bf16)
    g = pl.program_id(0)
    for j, early in enumerate((g < 2, (g == 0) | (g == 2))):

        @pl.when(early)
        def _():
            outs[2 * j][0] = out[:, j * half : (j + 1) * half]

        @pl.when(jnp.logical_not(early))
        def _():
            outs[2 * j + 1][0] = out[:, j * half : (j + 1) * half]


def weight_slabs(order, me, hidden, d, earlier=None, arrived=None, after=()):
    count, depth = hidden.shape[1] // 8, hidden.shape[0]
    part, width = d[0].shape
    targets = jnp.stack([me ^ r for r in order]).astype(jnp.int32)
    whole = pl.BlockSpec((part, width), lambda i, tab: (0, 0))
    in_specs = [pl.BlockSpec((depth, count), lambda i, tab: (0, tab[i])), whole, whole]
    slab = pl.BlockSpec((1, count, width), lambda i, tab: (i, 0, 0))
    more = [a for a in (earlier, arrived) if a is not None]
    if arrived is None:
        body, out_specs = functools.partial(slabs_body, earlier is not None), slab
        out_shape = jax.ShapeDtypeStruct((len(order), count, width), bf16)
    else:
        body = home_body
        piece = (1, count, width // 2)
        out_specs = [
            pl.BlockSpec(piece, lambda i, tab: (jnp.minimum(i, 1), 0, 0)),
            pl.BlockSpec(piece, lambda i, tab: (jnp.maximum(i - 2, 0), 0, 0)),
            pl.BlockSpec(piece, lambda i, tab: (jnp.minimum(i // 2, 1), 0, 0)),
            pl.BlockSpec(piece, lambda i, tab: (jnp.where(i == 3, 1, 0), 0, 0)),
        ]
        out_shape = [jax.ShapeDtypeStruct((2, count, width // 2), bf16)] * 4
    return pl.pallas_call(
        body,
        grid_spec=pltpu.PrefetchScalarGridSpec(
            num_scalar_prefetch=1, grid=(len(order),), in_specs=in_specs + [slab] * len(more) + any_specs(after), out_specs=out_specs
        ),
        out_shape=out_shape,
        compiler_params=params(dimension_semantics=("arbitrary",)),
        cost_estimate=cost(1 if earlier is None else 4 if arrived is None else 5),
        name="weight_slabs",
    )(targets, hidden, *d, *more, *after)


def add_body(a_ref, b_ref, out_ref):
    out_ref[...] = (a_ref[...].astype(f32) + b_ref[...].astype(f32)).astype(bf16)


def add_halves(first, second):
    def body(a_ref, b_ref, c_ref, d_ref, left_ref, right_ref):
        add_body(a_ref.at[0], b_ref.at[0], left_ref)
        add_body(c_ref.at[0], d_ref.at[0], right_ref)

    shape = first[0].shape[1:]
    block = pl.BlockSpec((1,) + shape, lambda i: (0, 0, 0))
    out = pl.BlockSpec(shape, lambda i: (0, 0))
    return pl.pallas_call(
        body,
        grid=(1,),
        in_specs=[block] * 4,
        out_specs=[out] * 2,
        out_shape=[jax.ShapeDtypeStruct(shape, bf16)] * 2,
        compiler_params=params(),
        cost_estimate=cost(1.4),
        name="add_halves",
    )(*first, *second)


def last_sum_body(left_ref, xa_ref, ya_ref, right_ref, yb_ref, xb_ref, out_ref):
    half = ya_ref.shape[1]
    for j, (mine, first, second) in enumerate(((left_ref, xa_ref, ya_ref), (right_ref, yb_ref, xb_ref))):
        total = mine[0].astype(f32) + first[0].astype(f32) + second[...].astype(f32)
        out_ref[:, j * half : (j + 1) * half] = total


def last_sum(left, xa, ya, right, yb, xb):
    rows, half = ya.shape
    tile = rows // 4
    block = pl.BlockSpec((1, tile, half), lambda i: (1, i, 0))
    flat = pl.BlockSpec((tile, half), lambda i: (i, 0))
    return pl.pallas_call(
        last_sum_body,
        grid=(4,),
        in_specs=[block, block, flat] * 2,
        out_specs=pl.BlockSpec((tile, 2 * half), lambda i: (i, 0)),
        out_shape=jax.ShapeDtypeStruct((rows, 2 * half), f32),
        compiler_params=params(dimension_semantics=("arbitrary",)),
        cost_estimate=cost(3),
        name="last_sum",
    )(left, xa, ya, right, yb, xb)


def stack_body(count, *refs):
    for i in range(count):
        refs[-1][i] = refs[i][...]


def stack(parts, after):
    return pl.pallas_call(
        functools.partial(stack_body, len(parts)),
        out_shape=jax.ShapeDtypeStruct((len(parts),) + parts[0].shape, parts[0].dtype),
        grid=(1,),
        in_specs=[whole_spec(a) for a in parts] + any_specs(after),
        out_specs=pl.BlockSpec((len(parts),) + parts[0].shape, lambda i: (0,) * (1 + parts[0].ndim)),
        compiler_params=params(),
        cost_estimate=cost(1),
        name="stack",
    )(*parts, *after)


def slab_body(mp_count, tab_ref, start_ref, *refs):
    count = mp_count - 1
    inner, outer = refs[:count], refs[count : 2 * count - 1]
    weight_ref, out_ref, held = refs[2 * count - 1 :]
    z = tab_ref[0]

    @pl.when(pl.program_id(0) == 0)
    def _():
        for k in range(1, mp_count):
            source = z ^ k
            by_partner = (source > z) == (z % 2 == 0)
            steps = jnp.abs(source - z)
            for u in range(1, mp_count):

                @pl.when(by_partner & (steps == u))
                def _():
                    held[k - 1] = inner[u - 1][...]

                if u < mp_count - 1:

                    @pl.when(jnp.logical_not(by_partner) & (steps == u))
                    def _():
                        held[k - 1] = outer[u - 1][...]

    out = start_ref[...]
    for k in range(count):
        shares_of = weight_ref[:, pl.ds(z ^ (k + 1), 1)]
        out = out + mm(held[k], shares_of.reshape(-1, shares_of.shape[-1]), NT)
    out_ref[...] = out.astype(bf16)


def slab_product(z, mp_count, start, inner, outer, weights):
    depth, width = start.shape
    tile = width // 4
    tab = z[None].astype(jnp.int32)
    rows = pl.BlockSpec(inner[0].shape, lambda g, tab: (0, 0))
    block = pl.BlockSpec((depth, tile), lambda g, tab: (0, g))
    return pl.pallas_call(
        functools.partial(slab_body, mp_count),
        grid_spec=pltpu.PrefetchScalarGridSpec(
            num_scalar_prefetch=1,
            grid=(4,),
            in_specs=[block]
            + [rows] * (len(inner) + len(outer))
            + [pl.BlockSpec((weights.shape[0] // 4,) + weights.shape[1:], lambda g, tab: (g, 0, 0, 0))],
            out_specs=block,
            scratch_shapes=[pltpu.VMEM((mp_count - 1,) + inner[0].shape, bf16)],
        ),
        out_shape=jax.ShapeDtypeStruct(start.shape, bf16),
        compiler_params=params(dimension_semantics=("arbitrary",)),
        cost_estimate=cost(1),
        name="slab_product",
    )(tab, start, *inner, *outer, weights)


def xor_pairs(count, mask):
    return [(i, i ^ mask) for i in range(count)]


def parts_body(count, after_count, tab_ref, top_ref, bottom_ref, weight_ref, *refs):
    k = pl.program_id(0)
    refs[after_count][0] = mm(top_ref[...], weight_ref[...], NT).astype(bf16)
    if count > 1:

        @pl.when(k == count - 1)
        def _():
            refs[-1][...] = mm(bottom_ref[...], weight_ref[...], NT)


def line_parts(d, weight, slabs, after=()):
    top, bottom = d
    rows, width = top.shape
    slab = weight.shape[0] // 4
    count = len(slabs)
    tab = jnp.stack(slabs).astype(jnp.int32)
    whole = pl.BlockSpec((rows, width), lambda k, tab: (0, 0))
    more = 1 if count > 1 else 0
    return pl.pallas_call(
        functools.partial(parts_body, count, len(after)),
        grid_spec=pltpu.PrefetchScalarGridSpec(
            num_scalar_prefetch=1,
            grid=(count,),
            in_specs=[whole, whole, pl.BlockSpec((slab, width), lambda k, tab: (tab[k], 0))] + any_specs(after),
            out_specs=[pl.BlockSpec((1, rows, slab), lambda k, tab: (k, 0, 0))]
            + [pl.BlockSpec((rows, slab), lambda k, tab: (0, 0))] * more,
        ),
        out_shape=[jax.ShapeDtypeStruct((count, rows, slab), bf16)] + [jax.ShapeDtypeStruct((rows, slab), f32)] * more,
        compiler_params=params(dimension_semantics=("arbitrary",)),
        cost_estimate=cost(1 + count),
        name="line_parts",
    )(tab, top, bottom, weight, *after)


def pass_body(masks, after_count, tab_ref, *refs):
    n = len(masks)
    z = tab_ref[0]
    at_end = (z == 0) | (z == 3)
    for got, part, out, mask in zip(refs[:n], refs[n : 2 * n], refs[2 * n + after_count :], masks):
        term = part[0].astype(f32)
        if mask == "ends":
            term = jnp.where(at_end, term, 0.0)
        elif mask == "middle":
            term = jnp.where(at_end, 0.0, term)
        out[...] = (got[...].astype(f32) + term).astype(bf16)


def pass_on(z, *jobs, after=()):
    shape = jobs[0][0].shape
    whole = pl.BlockSpec(shape, lambda i: (0, 0))
    part_specs = [pl.BlockSpec((1,) + shape, lambda i, k=job[2]: (k, 0, 0)) for job in jobs]
    return pl.pallas_call(
        functools.partial(pass_body, [job[3] for job in jobs], len(after)),
        grid=(1,),
        in_specs=[smem_spec()] + [whole] * len(jobs) + part_specs + any_specs(after),
        out_specs=[whole] * len(jobs),
        out_shape=[jax.ShapeDtypeStruct(shape, bf16)] * len(jobs),
        compiler_params=params(),
        cost_estimate=cost(1.5),
        name="pass_on",
    )(z[None].astype(jnp.int32), *[job[0] for job in jobs], *[job[1] for job in jobs], *after)


def line_start(d, weight, z, mp_count):
    (first,) = line_parts(d, weight, [z ^ 3])
    return [lax.ppermute(d[1], "mp", xor_pairs(mp_count, 1))], [lax.ppermute(d[1], "mp", [(1, 2), (2, 1)])], first


def line_steps(d, weight, z, mp_count, begun, before_parts=(), before_third=()):
    inner, outer, first = begun
    inner_swap = lambda a: lax.ppermute(a, "mp", xor_pairs(mp_count, 1))
    outer_swap = lambda a: lax.ppermute(a, "mp", [(1, 2), (2, 1)])
    (to_inner,) = pass_on(z, (outer[0], first, 0, "ends"), after=before_parts)
    to_outer = inner[0]
    parts, own_bottom = line_parts(d, weight, [z ^ 2, z ^ 1, z], (to_inner,))
    inner, outer, sent = inner + [inner_swap(to_inner)], outer + [outer_swap(to_outer)], []
    to_inner, to_outer = pass_on(z, (outer[1], parts, 0, "ends"), (inner[1], parts, 0, "middle"), after=before_third)
    sent.append(to_inner)
    inner, outer = inner + [inner_swap(to_inner)], outer + [outer_swap(to_outer)]
    to_inner, to_outer = pass_on(z, (outer[2], parts, 1, "all"), (inner[2], first, 0, "middle"))
    sent.append(to_inner)
    inner, outer = inner + [inner_swap(to_inner)], outer + [outer_swap(to_outer)]
    return parts, own_bottom, inner, outer, sent


def line_bottom(z, mp_count, begun, weights):
    _, own_bottom, inner, outer, _ = begun
    return slab_product(z, mp_count, own_bottom, inner[:3], outer[:2], weights)


def line_finish(begun, bottom):
    parts, _, inner, outer, _ = begun
    return joined(parts, inner[3], outer[3], bottom)


def joined_body(part_ref, a_ref, b_ref, bottom_ref, out_ref):
    rows = a_ref.shape[0]
    total = part_ref[0].astype(f32) + a_ref[...].astype(f32) + b_ref[...].astype(f32)
    out_ref[:rows, :] = total.astype(bf16)
    out_ref[rows:, :] = bottom_ref[...]


def joined(parts, a, b, bottom):
    rows, width = a.shape
    whole = pl.BlockSpec((rows, width), lambda i: (0, 0))
    return pl.pallas_call(
        joined_body,
        grid=(1,),
        in_specs=[pl.BlockSpec((1, rows, width), lambda i: (2, 0, 0)), whole, whole, whole],
        out_specs=pl.BlockSpec((2 * rows, width), lambda i: (0, 0)),
        out_shape=jax.ShapeDtypeStruct((2 * rows, width), bf16),
        compiler_params=params(),
        cost_estimate=cost(1.2),
        name="joined",
    )(parts, a, b, bottom)


def slots_of(ids, rel):
    place = jnp.arange(ids.shape[-1], dtype=jnp.int32)
    earlier = (rel[..., :, None] == rel[..., None, :]) & (place[None, :] < place[:, None])
    return rel * 2 + jnp.sum(earlier.astype(jnp.int32), axis=-1)


def tables_of(neg_blocks, me, z, dp_count, block_count):
    wanted = neg_blocks.reshape(-1)
    count = wanted.shape[0]
    neg_count = count // block_count
    place = jnp.arange(count, dtype=jnp.int32)
    slot = slots_of(wanted, (wanted // block_count) ^ me)
    hot = (slot[:, None] == place[None, :]).astype(jnp.int32)
    query_of = jnp.sum(hot * (place // neg_count)[:, None], axis=0)
    local_of = jnp.sum(hot * (wanted % block_count)[:, None], axis=0)
    tab = jnp.concatenate([query_of, local_of, z[None]]).astype(jnp.int32)
    rows_of = (wanted // block_count)[None, :] == jnp.arange(dp_count, dtype=jnp.int32)[:, None]
    rank = jnp.sum((rows_of[:, :, None] & (place[None, :, None] < place[None, None, :])).astype(jnp.int32), axis=1)
    local = jnp.where(rows_of, wanted % block_count, 0)
    asks = jnp.stack([jnp.sum(jnp.where(rank == k, local, 0), axis=1) for k in range(2)], axis=1)
    asked = lax.all_to_all(asks, "dp", 0, 0, tiled=True).reshape(-1)
    return tab, jnp.concatenate([asked, me[None]]).astype(jnp.int32)


def neighbours(query_hidden, passage_hidden, head_weight, neg_blocks, pos_ids):
    dp_count, mp_count = lax.axis_size("dp"), lax.axis_size("mp")
    me, z = lax.axis_index("dp"), lax.axis_index("mp")
    block_count = neg_blocks.shape[0]
    rows = query_hidden.shape[0] // block_count
    width = head_weight.shape[1]
    half = width // 2
    swap = lambda a, mask: lax.ppermute(a, "dp", xor_pairs(dp_count, mask))
    across = lambda a, mask: lax.ppermute(a, "mp", xor_pairs(mp_count, mask))

    slab = head_weight.shape[0] // mp_count
    share = lax.dynamic_index_in_dim(head_weight.reshape(mp_count, dp_count, slab // dp_count, width), me, 1, False)
    share = lax.all_to_all(share, "mp", 0, 0, tiled=True)
    ea = mm(passage_hidden, head_weight[:, :half], NN).astype(bf16)
    eb = mm(passage_hidden, head_weight[:, half:], NN).astype(bf16)
    eq = mm(query_hidden, head_weight, NN).astype(bf16)
    ax, by = swap(ea, 2), swap(eb, 4)
    ay, bx = swap(ea, 4), swap(eb, 2)
    ad, bd = swap(ax, 4), swap(by, 2)
    core = swap(stack([ea, eb], ()), 1)
    core_xy = swap(stack([ax, bx, ay, by], ()), 1)
    core_d = swap(stack([ad, bd], (eq,)), 1)
    sources = {
        0: [(ea, None), (eb, None)],
        1: [(core, 0), (core, 1)],
        2: [(ax, None), (bx, None)],
        3: [(core_xy, 0), (core_xy, 1)],
        4: [(ay, None), (by, None)],
        5: [(core_xy, 2), (core_xy, 3)],
        6: [(ad, None), (bd, None)],
        7: [(core_d, 0), (core_d, 1)],
    }
    tab, asked = tables_of(neg_blocks, me, z, dp_count, block_count)
    pos = pos_ids.reshape(block_count, rows)
    slots = slots_all(mp_count)
    sent = score_call(tuple(range(dp_count)), slots, rows, tab, eq, sources, ())
    parts = [sent[0]] + [across(sent[k], k) for k in range(1, mp_count)]
    mine = exp_call(slots, rows, tab, pos, parts, (asked,))
    tables = [mine] + [across(mine, k) for k in range(1, mp_count)]
    weights = lax.all_gather(stack([share], (sent[0],))[0], "dp", axis=0)

    *dq, loss = back_call(True, mp_count, rows, block_count, tab, pos, eq, tables, sources)
    query_begun = line_start(dq, head_weight, z, mp_count)
    own, here, to_x, to_y, to_d = back_call(
        False, mp_count, rows, block_count, tab, pos, eq, tables, sources, (dq[0],)
    )
    query_line = line_steps(dq, head_weight, z, mp_count, query_begun, (here,))
    away, home = (7, 3, 5, 1), (6, 2, 4, 0)
    away_q = weight_slabs(away, me, query_hidden, dq)
    home_q = weight_slabs(home, me, query_hidden, dq)
    query_bottom = line_bottom(z, mp_count, query_line, weights)
    got = [swap(to_x, 2), swap(to_y, 4), swap(to_d, 6)]
    other = swap(pack([here] + got, [query_line[2][-1], query_line[3][-1], away_q, home_q, asked, query_bottom]), 1)
    arrived = {}
    for i, a in enumerate([here] + got):
        arrived[2 * i], arrived[2 * i + 1] = (a, 0), (other, i)
    dp = gather_call(
        rows,
        block_count,
        asked,
        own,
        [arrived[r] for r in range(dp_count)],
        [],
    )
    passage_begun = line_start(dp, head_weight, z, mp_count)
    away_sum = weight_slabs(away, me, passage_hidden, dp, away_q, None, (passage_begun[-1],))
    query_grad = line_finish(query_line, query_bottom)
    passage_line = line_steps(dp, head_weight, z, mp_count, passage_begun, (away_sum,), (query_grad,))
    left, left_more, right, right_more = weight_slabs(home, me, passage_hidden, dp, home_q, swap(away_sum, 1))
    xa, yb = swap(left, 2), swap(right, 4)
    to_y, to_x = add_halves((left_more, xa), (right_more, yb))
    grad_weight = last_sum(left_more, xa, swap(to_y, 4), right_more, yb, swap(to_x, 2))
    passage_grad = line_finish(passage_line, line_bottom(z, mp_count, passage_line, weights))
    return loss.reshape(-1), grad_weight, query_grad, passage_grad


def back_norm(inverse, unit_rows, d_unit, inner):
    return (inverse[:, None] * (d_unit - unit_rows * inner[:, None])).astype(jnp.bfloat16)


def general(query_hidden, passage_hidden, head_weight, neg_blocks, pos_ids):
    dp_count = lax.axis_size("dp")
    block_count, neg_count = neg_blocks.shape
    row_count = query_hidden.shape[0]
    block_rows = row_count // block_count
    embed_width = head_weight.shape[1]
    cand_rows = (1 + neg_count) * block_rows
    request_count = block_count * neg_count
    slot_depth = (request_count + dp_count - 1) // dp_count
    slot_count = dp_count * slot_depth
    query_embed = jnp.dot(query_hidden, head_weight, preferred_element_type=jnp.float32)
    passage_embed = jnp.dot(passage_hidden, head_weight, preferred_element_type=jnp.float32)
    query_sq, passage_sq = lax.psum(
        (
            jnp.sum(query_embed * query_embed, axis=1),
            jnp.sum(passage_embed * passage_embed, axis=1),
        ),
        "mp",
    )
    query_inv = lax.rsqrt(query_sq + epsilon)
    passage_inv = lax.rsqrt(passage_sq + epsilon)
    query_unit = query_embed * query_inv[:, None]
    passage_unit = passage_embed * passage_inv[:, None]
    query_norm = query_unit.astype(jnp.bfloat16)
    passage_norm = passage_unit.astype(jnp.bfloat16)
    query_blocks = query_norm.reshape(block_count, block_rows, embed_width)
    passage_blocks = passage_norm.reshape(block_count, block_rows, embed_width)
    wanted = neg_blocks.reshape(-1)
    owners = wanted // block_count
    local_ids = wanted % block_count
    request_order = jnp.arange(request_count, dtype=jnp.int32)
    earlier_same = (owners[:, None] == owners[None, :]) & (
        request_order[None, :] < request_order[:, None]
    )
    owner_rank = jnp.sum(earlier_same.astype(jnp.int32), axis=1)
    slot_of = owners * slot_depth + owner_rank
    slot_table = (slot_of[:, None] == jnp.arange(slot_count, dtype=jnp.int32)[None, :]).astype(
        jnp.int32
    )
    requests = jnp.sum(slot_table * (local_ids + 1)[:, None], axis=0).reshape(dp_count, slot_depth)
    asked = lax.all_to_all(requests, "dp", split_axis=0, concat_axis=0, tiled=True).reshape(
        slot_count
    )
    live_slots = (asked > 0).astype(jnp.bfloat16)
    picked = jnp.take(passage_blocks, jnp.maximum(asked - 1, 0), axis=0) * live_slots[:, None, None]
    reply = picked.reshape(dp_count, slot_depth, block_rows, embed_width)
    arrived = lax.all_to_all(reply, "dp", split_axis=0, concat_axis=0, tiled=True).reshape(
        slot_count, block_rows, embed_width
    )
    fetched = jnp.take(arrived, slot_of, axis=0).reshape(
        block_count, neg_count, block_rows, embed_width
    )
    retrieved_documents = jnp.concatenate([passage_blocks[:, None], fetched], axis=1).reshape(
        block_count, cand_rows, embed_width
    )
    similarity_parts = jnp.einsum(
        "bqe,bce->bqc", query_blocks, retrieved_documents, preferred_element_type=jnp.float32
    )
    positions = pos_ids.reshape(block_count, block_rows)
    similarity_table = (
        lax.psum(similarity_parts.astype(jnp.bfloat16), "mp").astype(jnp.float32) / logit_divisor
    )
    columns = jnp.arange(cand_rows, dtype=jnp.int32)
    matching_document_slot = (columns[None, None, :] == positions[:, :, None]).astype(jnp.float32)
    exponent_values = jnp.exp(similarity_table)
    normalizer_totals = jnp.sum(exponent_values, axis=2)
    losses = jnp.log(normalizer_totals) - jnp.sum(similarity_table * matching_document_slot, axis=2)
    attention_probabilities = (
        (exponent_values / normalizer_totals[:, :, None] - matching_document_slot) / logit_divisor
    ).astype(jnp.bfloat16)
    d_query = jnp.einsum(
        "bqc,bce->bqe",
        attention_probabilities,
        retrieved_documents,
        preferred_element_type=jnp.float32,
    ).reshape(row_count, embed_width)
    d_cand = jnp.einsum(
        "bqc,bqe->bce", attention_probabilities, query_blocks, preferred_element_type=jnp.float32
    )
    own_terms = d_cand[:, :block_rows]
    neg_terms = (
        d_cand[:, block_rows:].reshape(request_count, block_rows, embed_width).astype(jnp.bfloat16)
    )
    outgoing = (
        jnp.zeros((slot_count, block_rows, embed_width), jnp.bfloat16).at[slot_of].set(neg_terms)
    )
    outgoing = outgoing.reshape(dp_count, slot_depth, block_rows, embed_width)
    returned = lax.all_to_all(outgoing, "dp", split_axis=0, concat_axis=0, tiled=True).reshape(
        slot_count, block_rows, embed_width
    )
    selector = (asked[None, :] - 1 == jnp.arange(block_count, dtype=jnp.int32)[:, None]).astype(
        jnp.bfloat16
    )
    d_passage = own_terms + jnp.einsum(
        "ls,sbe->lbe", selector, returned, preferred_element_type=jnp.float32
    )
    d_passage = d_passage.reshape(row_count, embed_width)
    query_inner, passage_inner = lax.psum(
        (jnp.sum(query_unit * d_query, axis=1), jnp.sum(passage_unit * d_passage, axis=1)), "mp"
    )
    d_query_embed = back_norm(query_inv, query_unit, d_query, query_inner)
    d_passage_embed = back_norm(passage_inv, passage_unit, d_passage, passage_inner)
    contract = (((0,), (0,)), ((), ()))
    query_part = lax.dot_general(
        query_hidden, d_query_embed, contract, preferred_element_type=jnp.float32
    )
    passage_part = lax.dot_general(
        passage_hidden, d_passage_embed, contract, preferred_element_type=jnp.float32
    )
    grad_weight = lax.psum_scatter(
        (query_part + passage_part).astype(jnp.bfloat16), "dp", scatter_dimension=0, tiled=True
    ).astype(jnp.float32)
    transpose_dims = (((1,), (1,)), ((), ()))
    query_back = lax.dot_general(
        d_query_embed, head_weight, transpose_dims, preferred_element_type=jnp.float32
    ).astype(jnp.bfloat16)
    passage_back = lax.dot_general(
        d_passage_embed, head_weight, transpose_dims, preferred_element_type=jnp.float32
    ).astype(jnp.bfloat16)
    query_grad, passage_grad = (
        lax.psum_scatter(query_back, "mp", scatter_dimension=1, tiled=True).astype(jnp.float32),
        lax.psum_scatter(passage_back, "mp", scatter_dimension=1, tiled=True).astype(jnp.float32),
    )
    return (
        losses.reshape(row_count),
        grad_weight,
        query_grad.astype(jnp.bfloat16),
        passage_grad.astype(jnp.bfloat16),
    )


def solution(mesh):
    placed = (P("dp", None), P("dp", None), P(None, "mp"), P("dp", None), P("dp"))
    sizes = dict(mesh.shape)

    def local(query_hidden, passage_hidden, head_weight, neg_blocks, pos_ids):
        exact = sizes["dp"] == 8 and sizes["mp"] == 4 and neg_blocks.shape == (4, 4)
        chosen = neighbours if exact else general
        return chosen(query_hidden, passage_hidden, head_weight, neg_blocks, pos_ids)

    return jax.shard_map(
        local,
        mesh=mesh,
        in_specs=placed,
        out_specs=(P("dp"), P("dp", "mp"), P("dp", "mp"), P("dp", "mp")),
        check_vma=False,
    )
```
